128 devices in a mesh: replica: 8 (over z, core), shard: 16 (over x, y).
Axes of the slice: x: 4, y: 4, z: 4, core: 2. Of those that a mesh axis runs over, the one named last changes fastest.
Arguments:
- grads: bfloat16 [8, 32, 1024, 1024], P('replica', 'shard')
- second_moment: float32 [32, 1024, 1024], P('shard', 'replica'), may hold values from 0.03 to 0.3
- left_stats: float32 [64, 1024, 1024], P('shard', 'replica')
- right_stats: float32 [64, 1024, 1024], P('shard', 'replica')
- left_root: bfloat16 [64, 1024, 1024], P('shard', 'replica'), as said below
- right_root: bfloat16 [64, 1024, 1024], P('shard', 'replica'), as said below
- owner_blocks: int32 [16, 4], replicated, may hold values from 0 to 32, as said below
Outputs:
- update: float32 [32, 1024, 1024], P('shard', 'replica')
- moment_new: float32 [32, 1024, 1024], P('shard', 'replica')
- left_new: float32 [64, 1024, 1024], P('shard', 'replica')
- right_new: float32 [64, 1024, 1024], P('shard', 'replica')
The draws below stay inside these ranges and needn't reach their ends.
Inputs may be any that keep to these rules, and one draw needn't show every extreme that they name: Every block number below 32 appears exactly once in owner_blocks; the value 32 marks an empty entry, and an owner's blocks come before its empty entries. Block b lies on shard device b // 2, and no owner's list holds two blocks of the same shard device. `right_root`: each 1024 x 1024 block is symmetric. `left_root`: each 1024 x 1024 block is symmetric.
All inputs are finite; a program needn't handle non-finite values.
Results may differ from the reference program's by a relative error of at most 0.0041.
Values may be sent and summed in bfloat16 or wider, within the bound.
A program may use at most 128 MiB of HBM per device.

```python
import math
import jax
import jax.numpy as jnp
from jax import lax

BS = 1024
K = 2
MOST = 4
NB = 32
SLOTS = 64
N_REPLICA = 8
N_SHARD = 16


def symmetric_blocks(key, diag_high, spread):
    noise_key, diag_key = jax.random.split(key)
    noise = jax.random.uniform(noise_key, (SLOTS, BS, BS), jnp.float32, -1.0, 1.0)
    offdiag = (noise + jnp.swapaxes(noise, 1, 2)) * (spread / math.sqrt(BS))
    diagonal = jnp.exp(jax.random.uniform(diag_key, (SLOTS, BS), jnp.float32, 0.0, math.log(diag_high)))
    identity = jnp.eye(BS, dtype=jnp.float32)
    return offdiag * (1.0 - identity) + identity * diagonal[:, :, None]


def draw_grads(key, part):
    key = jax.random.fold_in(key, 3)
    base_key, row_key, col_key = jax.random.split(key, 3)
    shape = (N_REPLICA, NB, BS, BS)
    factor = 3.0 / math.sqrt(BS * N_REPLICA)
    rising = jnp.exp(math.log(3.0) * jnp.arange(BS, dtype=jnp.float32) / BS)
    row_scale = jnp.exp(jax.random.uniform(row_key, (1, NB, BS, 1), jnp.float32, math.log(0.3), math.log(3.0))) * rising[None, None, :, None]
    col_scale = jnp.exp(jax.random.uniform(col_key, (1, NB, 1, BS), jnp.float32, math.log(0.3), math.log(3.0)))
    values = jax.random.normal(base_key, shape, jnp.float32)
    return (factor * values * row_scale * col_scale).astype(jnp.bfloat16)


def draw_left_stats(key, part):
    key = jax.random.fold_in(key, 5)
    return symmetric_blocks(key, 4.0, 1.0)


def draw_right_stats(key, part):
    key = jax.random.fold_in(key, 7)
    return symmetric_blocks(key, 4.0, 1.0)


def draw_left_root(key, part):
    key = jax.random.fold_in(key, 9)
    return symmetric_blocks(key, 4.0, 1.0).astype(jnp.bfloat16)


def draw_right_root(key, part):
    key = jax.random.fold_in(key, 13)
    return symmetric_blocks(key, 4.0, 1.0).astype(jnp.bfloat16)


def draw_owner_blocks(key, part):
    key = jax.random.fold_in(key, 11)
    split_key, order_key, source_key = jax.random.split(key, 3)
    halves = N_SHARD // 2
    leading = jax.random.randint(split_key, (halves,), 0, MOST + 1).astype(jnp.int32)
    leading = leading.at[0].set(MOST)
    paired = jnp.stack([leading, MOST - leading], axis=1).reshape(-1)
    order = jax.random.permutation(order_key, N_SHARD)
    counts = jnp.zeros((N_SHARD,), jnp.int32).at[order].set(paired)
    offsets = jnp.cumsum(counts) - counts
    entries = jnp.arange(MOST, dtype=jnp.int32)
    position = offsets[:, None] + entries[None, :]
    sources = jax.random.permutation(source_key, N_SHARD).astype(jnp.int32)
    block = sources[position % N_SHARD] * K + position // N_SHARD
    return jnp.where(entries[None, :] < counts[:, None], block, NB).astype(jnp.int32)


def shard_levels(stream_key, dims, cuts, smallest, high):
    loudness = 1.0
    for dim, shards_of in cuts:
        heights = jax.random.uniform(jax.random.fold_in(jax.random.fold_in(stream_key, 6), dim), (shards_of,), jnp.float32, smallest / len(cuts), high / len(cuts))
        loudness = loudness * jnp.repeat(jnp.exp(heights), dims[dim] // shards_of).reshape((-1,) + (1,) * (len(dims) - 1 - dim))
    return loudness


def setup_inputs(seed: int = 0) -> dict:
    splits = jax.random.split(jax.random.key(seed), 8)
    return {
        "grads": draw_grads(jax.random.fold_in(splits[7], 71), 0),
        "second_moment": jnp.clip(jnp.exp(math.log(0.3) - 2.3025852 * jax.random.uniform(splits[1], (NB, BS, BS), jnp.float32) ** shard_levels(splits[1], (NB, BS, BS), ((0, 16), (1, 8)), -0.2, 0.2)), 0.03, 0.3),
        "left_stats": draw_left_stats(jax.random.fold_in(splits[7], 71), 0),
        "right_stats": draw_right_stats(jax.random.fold_in(splits[7], 71), 0),
        "left_root": draw_left_root(jax.random.fold_in(splits[7], 71), 0),
        "right_root": draw_right_root(jax.random.fold_in(splits[7], 71), 0),
        "owner_blocks": draw_owner_blocks(jax.random.fold_in(splits[7], 71), 0),
    }


BETA_STAT = 0.99
BETA_MOMENT = 0.95
EPS_ADAM = 1e-08
EPS_NORM = 1e-06

def reference(grads, second_moment, left_stats, right_stats, left_root, right_root, owner_blocks):
    table = owner_blocks.reshape(-1).astype(jnp.int32)
    live = (table < NB).astype(jnp.float32)
    safe = jnp.minimum(table, NB - 1).astype(jnp.int32)

    def per_slot(items):
        index, alive, lstat, rstat, lroot, rroot = items
        picked = lax.dynamic_index_in_dim(grads, index, axis=1, keepdims=False)
        summed = lax.optimization_barrier(jnp.sum(picked.astype(jnp.float32), axis=0)) * alive
        rounded = summed.astype(jnp.bfloat16)
        left_out = BETA_STAT * lstat + (1.0 - BETA_STAT) * jnp.dot(rounded, rounded.T, preferred_element_type=jnp.float32)
        right_out = BETA_STAT * rstat + (1.0 - BETA_STAT) * jnp.dot(rounded.T, rounded, preferred_element_type=jnp.float32)
        product = jnp.dot(rounded, rroot, preferred_element_type=jnp.float32).astype(jnp.bfloat16)
        precond = jnp.dot(lroot, product, preferred_element_type=jnp.float32)
        return (left_out, right_out, precond)
    left_new, right_new, slot_precond = lax.map(per_slot, (safe, live, left_stats, right_stats, left_root, right_root))
    slot_of = jnp.argmax(table[None, :] == jnp.arange(NB, dtype=jnp.int32)[:, None], axis=1).astype(jnp.int32)
    precond = slot_precond[slot_of]
    gradient = lax.optimization_barrier(jnp.sum(grads, axis=0, dtype=jnp.float32))
    moment_new = BETA_MOMENT * second_moment + (1.0 - BETA_MOMENT) * gradient * gradient
    adam = gradient / (jnp.sqrt(moment_new) + EPS_ADAM)
    adam_norm = jnp.sqrt(lax.optimization_barrier(jnp.sum(adam * adam, axis=(1, 2))))
    pre_norm = jnp.sqrt(lax.optimization_barrier(jnp.sum(precond * precond, axis=(1, 2))))
    update = precond * (adam_norm / (pre_norm + EPS_NORM))[:, None, None]
    return (update, moment_new, left_new, right_new)
```

```python
import functools

import jax
import jax.numpy as jnp
from jax import lax
from jax.experimental import pallas as pl
from jax.experimental.pallas import tpu as pltpu
from jax.sharding import PartitionSpec as P

BETA_STAT = 0.99
BETA_MOMENT = 0.95
EPS_ADAM = 1e-08
EPS_NORM = 1e-06
MESH = pl.DeviceIdType.MESH

NS = 4
NK = 2
Q = 4


def flip(v, low, high):
    if low:
        v = v + 1 - 2 * (v % 2)
    if high:
        v = 3 - v
    return v


def gray_bits(v):
    return ((v + 1) // 2) % 2, v // 2


def kernel(
    ob_ref, inv_ref, grads, sm_hbm, lroot, rroot,
    update_out, moment_out, gl_out, gr_out,
    far0, far1, sm0, sm1, nr0, nr1, so, mg0, mg1, ms0, ms1, own0, own1, ownb,
    smv, mom, gf, rf, tb, pv, lh, nsend, nrecv,
    r_own, r_v0, r_sa, r_ra, r_sb, r_rb, r_sc, r_rc,
    l_own, l_v0, l_sa, l_ra, l_sb, l_rb, l_sc, l_rc,
    gl_h, gl_s, gl_r, gl_o, gr_h, gr_s, gr_r, gr_o,
    loc_sem, a_ss, a_rs, gag_ss, gag_rs, rag_ss, rag_rs,
    rp_ss, rp_rs, lp_ss, lp_rs, glp_ss, glp_rs, grp_ss, grp_rs, n_ss, n_rs,
):
    band = sm_hbm.shape[1]
    width = sm_hbm.shape[2]
    part = band // Q
    r = lax.axis_index("replica")
    s = lax.axis_index("shard")
    z, c = r // 2, r % 2
    x, y = s // 4, s % 4
    zp, zm, zf = (z + 1) % 4, (z + 3) % 4, (z + 2) % 4
    sib = 1 - c

    def dev(zz, cc):
        return (zz * 2 + cc, s)

    def rows(zz, cc):
        return pl.ds((zz * 2 + cc) * band, band)

    def shard_at(flips):
        return 4 * flip(x, 2 in flips, 3 in flips) + flip(y, 0 in flips, 1 in flips)

    def across(dim):
        return (r, shard_at((dim,)))

    def bits(shard):
        ya, yb = gray_bits(shard % 4)
        xa, xb = gray_bits(shard // 4)
        return (ya, yb, xa, xb)

    mine = bits(s)

    def remote(src, dst, ss, rs, to):
        return pltpu.make_async_remote_copy(
            src_ref=src, dst_ref=dst, send_sem=ss, recv_sem=rs, device_id=to, device_id_type=MESH
        )

    me = (r, s)

    def arrived(dst, ss, rs, to):
        remote(dst, dst, ss, rs, to).wait_recv()

    sends = []

    def go(cp):
        cp.start()
        sends.append(cp)

    locs = [
        pltpu.make_async_copy(grads.at[0, 0, rows(zm, c)], own0, loc_sem.at[0]),
        pltpu.make_async_copy(grads.at[0, 1, rows(zp, c)], own1, loc_sem.at[1]),
        pltpu.make_async_copy(grads.at[0, :, rows(z, c)], ownb, loc_sem.at[2]),
        pltpu.make_async_copy(sm_hbm, smv, loc_sem.at[3]),
        pltpu.make_async_copy(rroot, r_own, loc_sem.at[4]),
        pltpu.make_async_copy(lroot, l_own, loc_sem.at[5]),
    ]
    for cp in locs:
        cp.start()

    barrier = pltpu.get_barrier_semaphore()
    partners = [dev(z, sib)] + [dev(zz, cc) for zz in (zm, zp, zf) for cc in (0, 1)]
    partners += [across(d) for d in range(4)]
    for p in partners:
        pl.semaphore_signal(barrier, inc=1, device_id=p, device_id_type=MESH)
    pl.semaphore_wait(barrier, len(partners))

    for j in (0, 1):
        go(remote(grads.at[0, 0, rows(zf, j)], far0.at[c], a_ss.at[0, j], a_rs.at[0, c], dev(zm, j)))
        go(remote(grads.at[0, 1, rows(zf, j)], far1.at[c], a_ss.at[1, j], a_rs.at[1, c], dev(zp, j)))
    go(remote(grads.at[0, 0, rows(zm, sib)], sm0, a_ss.at[2, 0], a_rs.at[2, 0], dev(z, sib)))
    go(remote(grads.at[0, 1, rows(zp, sib)], sm1, a_ss.at[2, 1], a_rs.at[2, 1], dev(z, sib)))
    go(remote(grads.at[0, :, rows(z, sib)], so, a_ss.at[3, 0], a_rs.at[3, 0], dev(z, sib)))

    class Inward:
        def __init__(self, root, own, v0, sa, ra, sb, rb, sc, rc, ss, rs):
            self.root, self.own, self.v0 = root, own, v0
            self.bufs = [(sa, ra), (sb, rb), (sc, rc)]
            self.ss, self.rs = ss, rs

        def order(self, j):
            return [(j + i) % 4 for i in range(4)]

        def start(self):
            for j in range(Q):
                d = self.order(j)
                go(remote(self.root.at[:, pl.ds(part * j, part)], self.v0.at[j],
                          self.ss.at[0, j], self.rs.at[0, j], across(d[3])))

        def wait(self, stage):
            for j in range(Q):
                d = self.order(j)
                dst = self.v0.at[j] if stage == 0 else self.bufs[stage - 1][1].at[j]
                arrived(dst, self.ss.at[stage, j], self.rs.at[stage, j], across(d[3 - stage]))

        def pick(self, j, level, home_flips, k, ea, eb):
            d = self.order(j)
            place = inv_ref[2 * shard_at(home_flips) + k]
            owner, slot = place // NS, place % NS
            theirs = bits(owner)
            value = jnp.where(theirs[d[3]] != mine[d[3]], self.v0[j, slot],
                              self.own[slot, pl.ds(part * j, part)])
            if level >= 1:
                value = jnp.where(theirs[d[2]] != mine[d[2]], self.bufs[0][1][j, ea], value)
            if level >= 2:
                value = jnp.where(theirs[d[1]] != mine[d[1]], self.bufs[1][1][j, eb], value)
            if level >= 3:
                value = jnp.where(theirs[d[0]] != mine[d[0]], self.bufs[2][1][j, k], value)
            return value

        def send(self, stage):
            src, dst = self.bufs[stage - 1]
            for j in range(Q):
                d = self.order(j)
                for e in range(8 >> (stage - 1)):
                    k, r0, r1 = e % 2, (e // 2) % 2, e // 4
                    if stage == 1:
                        flips = (d[2],) + ((d[0],) if r0 else ()) + ((d[1],) if r1 else ())
                        ea = eb = None
                    elif stage == 2:
                        flips = (d[1],) + ((d[0],) if r0 else ())
                        ea, eb = 4 + 2 * r0 + k, None
                    else:
                        flips = (d[0],)
                        ea, eb = 2 + k, 2 + k
                    src[j, e] = self.pick(j, stage - 1, flips, k, ea, eb)
                go(remote(src.at[j], dst.at[j], self.ss.at[stage, j], self.rs.at[stage, j], across(d[3 - stage])))

        def finish(self, put):
            for j in range(Q):
                for k in range(NK):
                    put(j, k, self.pick(j, 3, (), k, k, k))

    right = Inward(rroot, r_own, r_v0, r_sa, r_ra, r_sb, r_rb, r_sc, r_rc, rp_ss, rp_rs)
    left = Inward(lroot, l_own, l_v0, l_sa, l_ra, l_sb, l_rb, l_sc, l_rc, lp_ss, lp_rs)
    right.start()
    left.start()

    for j in (0, 1):
        go(remote(grads.at[0, 1, rows(zm, j)], nr1.at[c], a_ss.at[4, j], a_rs.at[4, c], dev(zm, j)))
        go(remote(grads.at[0, 0, rows(zp, j)], nr0.at[c], a_ss.at[5, j], a_rs.at[5, c], dev(zp, j)))

    locs[4].wait()
    right.wait(0)
    right.send(1)

    for cc in (0, 1):
        arrived(far0.at[cc], a_ss.at[0, cc], a_rs.at[0, cc], dev(zm, cc))
        arrived(far1.at[cc], a_ss.at[1, cc], a_rs.at[1, cc], dev(zp, cc))
    arrived(sm0, a_ss.at[2, 0], a_rs.at[2, 0], dev(z, sib))
    arrived(sm1, a_ss.at[2, 1], a_rs.at[2, 1], dev(z, sib))
    locs[0].wait()
    locs[1].wait()
    step_rows = 16

    def f32(v):
        return v.astype(jnp.float32)

    @pl.loop(0, band // step_rows)
    def _(i):
        at = pl.ds(pl.multiple_of(i * step_rows, step_rows), step_rows)
        ms0[at] = (f32(own0[at]) + f32(sm0[at])) + (f32(far0[0, at]) + f32(far0[1, at]))
        ms1[at] = (f32(own1[at]) + f32(sm1[at])) + (f32(far1[0, at]) + f32(far1[1, at]))

    go(remote(ms0, mg0, a_ss.at[6, 0], a_rs.at[6, 0], dev(zm, c)))
    go(remote(ms1, mg1, a_ss.at[6, 1], a_rs.at[6, 1], dev(zp, c)))

    locs[5].wait()
    left.wait(0)
    left.send(1)
    right.wait(1)
    right.send(2)

    for cc in (0, 1):
        arrived(nr1.at[cc], a_ss.at[4, cc], a_rs.at[4, cc], dev(zm, cc))
        arrived(nr0.at[cc], a_ss.at[5, cc], a_rs.at[5, cc], dev(zp, cc))
    arrived(so, a_ss.at[3, 0], a_rs.at[3, 0], dev(z, sib))
    locs[2].wait()
    locs[3].wait()
    arrived(mg0, a_ss.at[6, 0], a_rs.at[6, 0], dev(zm, c))
    arrived(mg1, a_ss.at[6, 1], a_rs.at[6, 1], dev(zp, c))

    def fold(v):
        v = v[:8] + v[8:]
        total = v[:, :128]
        for i in range(1, width // 128):
            total = total + v[:, 128 * i:128 * (i + 1)]
        return total

    for k, near, merged in ((0, nr0, mg0), (1, nr1, mg1)):
        def one(i, acc, k=k, near=near, merged=merged):
            start = pl.multiple_of(i * step_rows, step_rows)
            at = pl.ds(start, step_rows)
            g = (f32(ownb[k, at]) + f32(so[k, at])) + (f32(near[0, at]) + f32(near[1, at])) + merged[at]
            m = BETA_MOMENT * smv[k, at] + (1.0 - BETA_MOMENT) * g * g
            mom[k, at] = m
            a = g / (jnp.sqrt(m) + EPS_ADAM)
            gf[k, pl.ds(pl.multiple_of(r * band + start, step_rows), step_rows)] = g.astype(jnp.bfloat16)
            return acc + fold(a * a)

        nsend[k] = lax.fori_loop(0, band // step_rows, one, jnp.zeros((8, 128), jnp.float32))

    class Gather:
        def __init__(self, buf, ss, rs):
            self.buf, self.ss, self.rs = buf, ss, rs

        def copy(self, i, k, zz, cc, to):
            piece = self.buf.at[k, rows(zz, cc)]
            return remote(piece, piece, self.ss.at[i], self.rs.at[i], to)

        def got(self, i, k, zz, cc, to):
            self.copy(i, k, zz, cc, to).wait_recv()

        def start(self):
            go(self.copy(0, 0, z, c, dev(zm, c)))
            go(self.copy(1, 1, z, c, dev(zp, c)))
            go(self.copy(2, 1, z, c, dev(zm, c)))
            go(self.copy(3, 0, z, c, dev(zp, c)))
            go(self.copy(4, 0, z, c, dev(z, sib)))
            go(self.copy(5, 1, z, c, dev(z, sib)))

        def forward(self):
            self.got(0, 0, zp, c, dev(zm, c))
            go(self.copy(6, 0, zp, c, dev(zm, c)))
            self.got(1, 1, zm, c, dev(zp, c))
            go(self.copy(7, 1, zm, c, dev(zp, c)))
            go(self.copy(8, 0, zp, c, dev(z, sib)))
            go(self.copy(9, 1, zm, c, dev(z, sib)))

        def rest(self):
            self.got(2, 1, zp, c, dev(zm, c))
            go(self.copy(10, 1, zp, c, dev(z, sib)))
            self.got(3, 0, zm, c, dev(zp, c))
            go(self.copy(11, 0, zm, c, dev(z, sib)))

        def last(self):
            self.got(6, 0, zf, c, dev(zm, c))
            go(self.copy(12, 0, zf, c, dev(z, sib)))
            self.got(7, 1, zf, c, dev(zp, c))
            go(self.copy(13, 1, zf, c, dev(z, sib)))

        def complete(self):
            for i, k, zz in ((4, 0, z), (5, 1, z), (8, 0, zp), (9, 1, zm), (10, 1, zp), (11, 0, zm), (12, 0, zf), (13, 1, zf)):
                self.got(i, k, zz, sib, dev(z, sib))

    gather_g = Gather(gf, gag_ss, gag_rs)
    gather_r = Gather(rf, rag_ss, rag_rs)
    gather_g.start()
    mom_cp = pltpu.make_async_copy(mom, moment_out, loc_sem.at[6])
    mom_cp.start()

    left.wait(1)
    left.send(2)
    right.wait(2)
    right.send(3)
    gather_g.forward()
    left.wait(2)
    left.send(3)
    gather_g.rest()
    right.wait(3)

    def put_right(j, k, value):
        rf[k, pl.ds(pl.multiple_of(r * band + part * j, part), part)] = value

    right.finish(put_right)
    gather_g.last()
    gather_r.start()
    gather_g.complete()

    class Outward:
        def __init__(self, held, src, dst, out, ss, rs):
            self.held, self.src, self.dst, self.out, self.ss, self.rs = held, src, dst, out, ss, rs

        def order(self, j):
            return [(j + i) % 4 for i in range(4)]

        def spread(self, stage):
            n = 2 << stage
            for j in range(Q):
                d = self.order(j)
                go(remote(self.held.at[j, pl.ds(0, n)], self.held.at[j, pl.ds(n, n)],
                          self.ss.at[stage, j], self.rs.at[stage, j], across(d[stage])))

        def wait(self, stage):
            n = 2 << stage
            for j in range(Q):
                d = self.order(j)
                dst = self.dst.at[j] if stage == 3 else self.held.at[j, pl.ds(n, n)]
                arrived(dst, self.ss.at[stage, j], self.rs.at[stage, j], across(d[stage]))

        def look(self, j, owner, q):
            d = self.order(j)
            block = ob_ref[owner * NS + q]
            safe = jnp.minimum(block, 31)
            theirs = bits(safe // 2)
            differ = [jnp.where(theirs[t] != mine[t], 1, 0) for t in d]
            entry = 2 * (differ[0] + 2 * differ[1] + 4 * differ[2]) + safe % 2
            return block, differ[3], self.held[j, entry]

        def send(self):
            for j in range(Q):
                d = self.order(j)
                for q in range(NS):
                    self.src[j, q] = self.look(j, shard_at((d[3],)), q)[2]
                go(remote(self.src.at[j], self.dst.at[j], self.ss.at[3, j], self.rs.at[3, j], across(d[3])))

        def finish(self):
            for j in range(Q):
                for q in range(NS):
                    block, far, here = self.look(j, s, q)
                    value = jnp.where(far == 1, self.dst[j, q], here)
                    value = jnp.where(block < 32, value, jnp.zeros_like(value))
                    self.out[q, pl.ds(part * j, part)] = value

    out_l = Outward(gl_h, gl_s, gl_r, gl_o, glp_ss, glp_rs)
    out_r = Outward(gr_h, gr_s, gr_r, gr_o, grp_ss, grp_rs)

    tile = 256
    mm = functools.partial(lax.dot_general, preferred_element_type=jnp.float32)
    for k in range(NK):
        band_rows = gf[k, pl.ds(pl.multiple_of(r * band, band), band)]

        @pl.loop(0, width // tile)
        def _(i, k=k, band_rows=band_rows):
            at = pl.ds(pl.multiple_of(i * tile, tile), tile)
            g = mm(band_rows, gf[k, at], (((1,), (1,)), ((), ()))).astype(jnp.bfloat16)
            for j in range(Q):
                gl_h[j, k, :, at] = g[part * j:part * (j + 1)]

    out_l.spread(0)
    for k in range(NK):
        cols = gf[k, :, pl.ds(pl.multiple_of(r * band, band), band)].T

        @pl.loop(0, width // tile)
        def _(i, k=k, cols=cols):
            at = pl.ds(pl.multiple_of(i * tile, tile), tile)
            g = mm(cols, gf[k, :, at], (((1,), (0,)), ((), ()))).astype(jnp.bfloat16)
            for j in range(Q):
                gr_h[j, k, :, at] = g[part * j:part * (j + 1)]

    out_r.spread(0)

    left.wait(3)

    def put_left(j, k, value):
        lh[k, pl.ds(part * j, part)] = value

    left.finish(put_left)

    out_l.wait(0)
    out_l.spread(1)
    out_r.wait(0)
    out_r.spread(1)
    gather_r.forward()
    out_l.wait(1)
    out_l.spread(2)
    gather_r.rest()
    gather_r.last()
    out_r.wait(1)
    out_r.spread(2)
    gather_r.complete()

    for k in range(NK):
        @pl.loop(0, width // tile)
        def _(i, k=k):
            at = pl.ds(pl.multiple_of(i * tile, tile), tile)
            tb[at] = mm(gf[k, at], rf[k], (((1,), (0,)), ((), ()))).astype(jnp.bfloat16)

        @pl.loop(0, width // tile)
        def _(i, k=k):
            at = pl.ds(pl.multiple_of(i * tile, tile), tile)
            pv[k, :, at] = mm(lh[k], tb[:, at], (((1,), (0,)), ((), ())))

        def square(i, acc, k=k):
            v = pv[k, pl.ds(pl.multiple_of(i * step_rows, step_rows), step_rows)]
            return acc + fold(v * v)

        nsend[NK + k] = lax.fori_loop(0, band // step_rows, square, jnp.zeros((8, 128), jnp.float32))

    others = [(z, sib, 0)] + [(zz, cc, 1 + 2 * i + cc) for i, zz in enumerate((zm, zp, zf)) for cc in (0, 1)]
    for zz, cc, i in others:
        go(remote(nsend, nrecv.at[r], n_ss.at[i], n_rs.at[r], dev(zz, cc)))
    for zz, cc, i in others:
        src = zz * 2 + cc
        arrived(nrecv.at[src], n_ss.at[i], n_rs.at[src], dev(zz, cc))
    nrecv[r] = nsend[...]
    sums = nrecv[0]
    for i in range(1, 8):
        sums = sums + nrecv[i]
    for k in range(NK):
        adam_total = jnp.sum(sums[k], keepdims=True)
        pre_total = jnp.sum(sums[NK + k], keepdims=True)
        scaling = jnp.sqrt(adam_total) / (jnp.sqrt(pre_total) + EPS_NORM)

        @pl.loop(0, band // step_rows)
        def _(i, k=k, scaling=scaling):
            at = pl.ds(pl.multiple_of(i * step_rows, step_rows), step_rows)
            pv[k, at] = pv[k, at] * scaling

    up_cp = pltpu.make_async_copy(pv, update_out, loc_sem.at[7])
    up_cp.start()

    out_l.wait(2)
    out_l.send()
    out_r.wait(2)
    out_r.send()
    out_l.wait(3)
    out_l.finish()
    gl_cp = pltpu.make_async_copy(gl_o, gl_out, loc_sem.at[8])
    gl_cp.start()
    out_r.wait(3)
    out_r.finish()
    gr_cp = pltpu.make_async_copy(gr_o, gr_out, loc_sem.at[9])
    gr_cp.start()

    for cp in sends:
        cp.wait_send()
    for cp in (mom_cp, up_cp, gl_cp, gr_cp):
        cp.wait()


def body(grads, second_moment, left_stats, right_stats, left_root, right_root, owner_blocks):
    bf16, f32 = jnp.bfloat16, jnp.float32
    band, width = second_moment.shape[1], second_moment.shape[2]
    full = 8 * band
    part = band // Q
    table = owner_blocks.reshape(-1)
    blocks = jnp.arange(32, dtype=jnp.int32)
    inverse = jnp.sum(
        jnp.where(table[None, :] == blocks[:, None], jnp.arange(64, dtype=jnp.int32)[None, :], 0), axis=1
    )
    V, D = pltpu.VMEM, pltpu.SemaphoreType.DMA
    inward = [
        V((NS, band, width), bf16), V((Q, NS, part, width), bf16),
        V((Q, 8, part, width), bf16), V((Q, 8, part, width), bf16),
        V((Q, 4, part, width), bf16), V((Q, 4, part, width), bf16),
        V((Q, 2, part, width), bf16), V((Q, 2, part, width), bf16),
    ]
    outward = [
        V((Q, 16, part, width), bf16), V((Q, NS, part, width), bf16),
        V((Q, NS, part, width), bf16), V((NS, band, width), bf16),
    ]
    scratch = (
        [V((2, band, width), bf16)] * 2
        + [V((band, width), bf16)] * 2
        + [V((2, band, width), bf16)] * 2
        + [V((2, band, width), bf16)]
        + [V((band, width), f32)] * 4
        + [V((band, width), bf16)] * 2
        + [V((2, band, width), bf16)]
        + [V((2, band, width), f32)] * 2
        + [V((2, full, width), bf16)] * 2
        + [V((full, width), bf16)]
        + [V((2, band, width), f32)]
        + [V((2, band, width), bf16)]
        + [V((4, 8, 128), f32), V((8, 4, 8, 128), f32)]
        + inward + inward + outward + outward
        + [D((10,)), D((7, 2)), D((7, 2)), D((14,)), D((14,)), D((14,)), D((14,))]
        + [D((4, Q))] * 8
        + [D((7,)), D((8,))]
    )
    hbm = pl.BlockSpec(memory_space=pl.ANY)
    smem = pl.BlockSpec(memory_space=pltpu.SMEM)
    update, moment_new, gram_left, gram_right = pl.pallas_call(
        kernel,
        out_shape=(
            jax.ShapeDtypeStruct((2, band, width), f32),
            jax.ShapeDtypeStruct((2, band, width), f32),
            jax.ShapeDtypeStruct((NS, band, width), bf16),
            jax.ShapeDtypeStruct((NS, band, width), bf16),
        ),
        in_specs=[smem, smem, hbm, hbm, hbm, hbm],
        out_specs=(hbm, hbm, hbm, hbm),
        scratch_shapes=scratch,
        compiler_params=pltpu.CompilerParams(
            collective_id=0, has_side_effects=True, vmem_limit_bytes=60 * 2**20
        ),
        name="shampoo",
    )(table, inverse, grads, second_moment, left_root, right_root)
    left_new = BETA_STAT * left_stats + (1.0 - BETA_STAT) * gram_left.astype(f32)
    right_new = BETA_STAT * right_stats + (1.0 - BETA_STAT) * gram_right.astype(f32)
    return (update, moment_new, left_new, right_new)


def solution(mesh):
    in_specs = (
        P("replica", "shard", None, None),
        P("shard", "replica", None),
        P("shard", "replica", None),
        P("shard", "replica", None),
        P("shard", "replica", None),
        P("shard", "replica", None),
        P(),
    )
    out_specs = (
        P("shard", "replica", None),
        P("shard", "replica", None),
        P("shard", "replica", None),
        P("shard", "replica", None),
    )
    return jax.shard_map(body, mesh=mesh, in_specs=in_specs, out_specs=out_specs, check_vma=False)
```

```python
import functools

import jax
import jax.numpy as jnp
from jax import lax
from jax.experimental import pallas as pl
from jax.experimental.pallas import tpu as pltpu
from jax.sharding import PartitionSpec as P

BETA_STAT = 0.99
BETA_MOMENT = 0.95
EPS_ADAM = 1e-08
EPS_NORM = 1e-06
MESH = pl.DeviceIdType.MESH

NS = 4
NK = 2
Q = 4
TILES = (0, 1, -2, 3, 4)
SWAPPED = (1, 2, 3)
TILE = 128


def flip(v, low, high):
    if low:
        v = v + 1 - 2 * (v % 2)
    if high:
        v = 3 - v
    return v


def gray_bits(v):
    return ((v + 1) // 2) % 2, v // 2


def kernel(
    ob_ref, inv_ref, grads, sm_hbm, lroot, rroot,
    update_out, moment_out, gl_out, gr_out,
    far0, far1, sm0, sm1, nr0, nr1, so, mg0, mg1, ms0, ms1, own0, own1, ownb,
    smv, mom, gf, rf, tb, pv, lh, nsend, nrecv,
    r_own, r_v0, r_sa, r_ra, r_sb, r_rb, r_sc, r_rc,
    l_own, l_v0, l_sa, l_ra, l_sb, l_rb, l_sc, l_rc,
    gl_h, gl_s, gl_r, gl_o, gl_xs, gl_xr, gr_h, gr_s, gr_r, gr_o, gr_xs, gr_xr,
    loc_sem, a_ss, a_rs, gag_ss, gag_rs, rag_ss, rag_rs,
    rp_ss, rp_rs, lp_ss, lp_rs, glp_ss, glp_rs, grp_ss, grp_rs, xl_ss, xl_rs, xr_ss, xr_rs, n_ss, n_rs,
):
    band = sm_hbm.shape[1]
    width = sm_hbm.shape[2]
    part = band // Q
    r = lax.axis_index("replica")
    s = lax.axis_index("shard")
    z, c = r // 2, r % 2
    x, y = s // 4, s % 4
    zp, zm, zf = (z + 1) % 4, (z + 3) % 4, (z + 2) % 4
    sib = 1 - c

    def dev(zz, cc):
        return (zz * 2 + cc, s)

    def rows(zz, cc):
        return pl.ds((zz * 2 + cc) * band, band)

    def shard_at(flips):
        return 4 * flip(x, 2 in flips, 3 in flips) + flip(y, 0 in flips, 1 in flips)

    def across(dim):
        return (r, shard_at((dim,)))

    def bits(shard):
        ya, yb = gray_bits(shard % 4)
        xa, xb = gray_bits(shard // 4)
        return (ya, yb, xa, xb)

    mine = bits(s)

    def remote(src, dst, ss, rs, to):
        return pltpu.make_async_remote_copy(
            src_ref=src, dst_ref=dst, send_sem=ss, recv_sem=rs, device_id=to, device_id_type=MESH
        )

    me = (r, s)

    def arrived(dst, ss, rs, to):
        remote(dst, dst, ss, rs, to).wait_recv()

    sends = []

    def go(cp):
        cp.start()
        sends.append(cp)

    locs = [
        pltpu.make_async_copy(grads.at[0, 0, rows(zm, c)], own0, loc_sem.at[0]),
        pltpu.make_async_copy(grads.at[0, 1, rows(zp, c)], own1, loc_sem.at[1]),
        pltpu.make_async_copy(grads.at[0, :, rows(z, c)], ownb, loc_sem.at[2]),
        pltpu.make_async_copy(sm_hbm, smv, loc_sem.at[3]),
        pltpu.make_async_copy(rroot, r_own, loc_sem.at[4]),
        pltpu.make_async_copy(lroot, l_own, loc_sem.at[5]),
    ]
    for cp in locs:
        cp.start()

    barrier = pltpu.get_barrier_semaphore()
    partners = [dev(z, sib)] + [dev(zz, cc) for zz in (zm, zp, zf) for cc in (0, 1)]
    partners += [across(d) for d in range(4)]
    for p in partners:
        pl.semaphore_signal(barrier, inc=1, device_id=p, device_id_type=MESH)
    pl.semaphore_wait(barrier, len(partners))

    for j in (0, 1):
        go(remote(grads.at[0, 0, rows(zf, j)], far0.at[c], a_ss.at[0, j], a_rs.at[0, c], dev(zm, j)))
        go(remote(grads.at[0, 1, rows(zf, j)], far1.at[c], a_ss.at[1, j], a_rs.at[1, c], dev(zp, j)))
    go(remote(grads.at[0, 0, rows(zm, sib)], sm0, a_ss.at[2, 0], a_rs.at[2, 0], dev(z, sib)))
    go(remote(grads.at[0, 1, rows(zp, sib)], sm1, a_ss.at[2, 1], a_rs.at[2, 1], dev(z, sib)))
    go(remote(grads.at[0, :, rows(z, sib)], so, a_ss.at[3, 0], a_rs.at[3, 0], dev(z, sib)))

    class Inward:
        def __init__(self, root, own, v0, sa, ra, sb, rb, sc, rc, ss, rs):
            self.root, self.own, self.v0 = root, own, v0
            self.bufs = [(sa, ra), (sb, rb), (sc, rc)]
            self.ss, self.rs = ss, rs

        def order(self, j):
            return [(j + i) % 4 for i in range(4)]

        def start(self):
            for j in range(Q):
                d = self.order(j)
                go(remote(self.root.at[:, pl.ds(part * j, part)], self.v0.at[j],
                          self.ss.at[0, j], self.rs.at[0, j], across(d[3])))

        def wait(self, stage):
            for j in range(Q):
                d = self.order(j)
                dst = self.v0.at[j] if stage == 0 else self.bufs[stage - 1][1].at[j]
                arrived(dst, self.ss.at[stage, j], self.rs.at[stage, j], across(d[3 - stage]))

        def pick(self, j, level, home_flips, k, ea, eb):
            d = self.order(j)
            place = inv_ref[2 * shard_at(home_flips) + k]
            owner, slot = place // NS, place % NS
            theirs = bits(owner)
            value = jnp.where(theirs[d[3]] != mine[d[3]], self.v0[j, slot],
                              self.own[slot, pl.ds(part * j, part)])
            if level >= 1:
                value = jnp.where(theirs[d[2]] != mine[d[2]], self.bufs[0][1][j, ea], value)
            if level >= 2:
                value = jnp.where(theirs[d[1]] != mine[d[1]], self.bufs[1][1][j, eb], value)
            if level >= 3:
                value = jnp.where(theirs[d[0]] != mine[d[0]], self.bufs[2][1][j, k], value)
            return value

        def send(self, stage):
            src, dst = self.bufs[stage - 1]
            for j in range(Q):
                d = self.order(j)
                for e in range(8 >> (stage - 1)):
                    k, r0, r1 = e % 2, (e // 2) % 2, e // 4
                    if stage == 1:
                        flips = (d[2],) + ((d[0],) if r0 else ()) + ((d[1],) if r1 else ())
                        ea = eb = None
                    elif stage == 2:
                        flips = (d[1],) + ((d[0],) if r0 else ())
                        ea, eb = 4 + 2 * r0 + k, None
                    else:
                        flips = (d[0],)
                        ea, eb = 2 + k, 2 + k
                    src[j, e] = self.pick(j, stage - 1, flips, k, ea, eb)
                go(remote(src.at[j], dst.at[j], self.ss.at[stage, j], self.rs.at[stage, j], across(d[3 - stage])))

        def finish(self, put):
            for j in range(Q):
                for k in range(NK):
                    put(j, k, self.pick(j, 3, (), k, k, k))

    right = Inward(rroot, r_own, r_v0, r_sa, r_ra, r_sb, r_rb, r_sc, r_rc, rp_ss, rp_rs)
    left = Inward(lroot, l_own, l_v0, l_sa, l_ra, l_sb, l_rb, l_sc, l_rc, lp_ss, lp_rs)
    right.start()
    left.start()

    def near_send(j, there):
        go(remote(grads.at[0, 1, rows(zm, there)], nr1.at[c], a_ss.at[4, j], a_rs.at[4, c], dev(zm, there)))
        go(remote(grads.at[0, 0, rows(zp, there)], nr0.at[c], a_ss.at[5, j], a_rs.at[5, c], dev(zp, there)))

    near_send(0, c)
    locs[4].wait()
    right.wait(0)
    right.send(1)

    for cc in (0, 1):
        arrived(far0.at[cc], a_ss.at[0, cc], a_rs.at[0, cc], dev(zm, cc))
        arrived(far1.at[cc], a_ss.at[1, cc], a_rs.at[1, cc], dev(zp, cc))
    near_send(1, sib)
    arrived(sm0, a_ss.at[2, 0], a_rs.at[2, 0], dev(z, sib))
    arrived(sm1, a_ss.at[2, 1], a_rs.at[2, 1], dev(z, sib))
    locs[0].wait()
    locs[1].wait()
    step_rows = 16

    def f32(v):
        return v.astype(jnp.float32)

    half = band // 2
    halves = [pl.ds(0, half), pl.ds(half, half)]
    for h in (0, 1):
        @pl.loop(0, half // step_rows)
        def _(i, h=h):
            at = pl.ds(pl.multiple_of(h * half + i * step_rows, step_rows), step_rows)
            ms0[at] = (f32(own0[at]) + f32(sm0[at])) + (f32(far0[0, at]) + f32(far0[1, at]))
            ms1[at] = (f32(own1[at]) + f32(sm1[at])) + (f32(far1[0, at]) + f32(far1[1, at]))

        at = halves[h]
        go(remote(ms0.at[at], mg0.at[at], a_ss.at[6 + h, 0], a_rs.at[6 + h, 0], dev(zm, c)))
        go(remote(ms1.at[at], mg1.at[at], a_ss.at[6 + h, 1], a_rs.at[6 + h, 1], dev(zp, c)))

    locs[5].wait()
    left.wait(0)
    left.send(1)
    right.wait(1)
    right.send(2)

    for cc in (0, 1):
        arrived(nr1.at[cc], a_ss.at[4, cc], a_rs.at[4, cc], dev(zm, cc))
        arrived(nr0.at[cc], a_ss.at[5, cc], a_rs.at[5, cc], dev(zp, cc))
    arrived(so, a_ss.at[3, 0], a_rs.at[3, 0], dev(z, sib))
    locs[2].wait()
    locs[3].wait()
    def fold(v):
        v = v[:8] + v[8:]
        total = v[:, :128]
        for i in range(1, width // 128):
            total = total + v[:, 128 * i:128 * (i + 1)]
        return total

    def gradient(h):
        at = halves[h]
        arrived(mg0.at[at], a_ss.at[6 + h, 0], a_rs.at[6 + h, 0], dev(zm, c))
        arrived(mg1.at[at], a_ss.at[6 + h, 1], a_rs.at[6 + h, 1], dev(zp, c))
        for k, near, merged in ((0, nr0, mg0), (1, nr1, mg1)):
            def one(i, acc, k=k, near=near, merged=merged):
                start = pl.multiple_of(h * half + i * step_rows, step_rows)
                at = pl.ds(start, step_rows)
                g = (f32(ownb[k, at]) + f32(so[k, at])) + (f32(near[0, at]) + f32(near[1, at])) + merged[at]
                m = BETA_MOMENT * smv[k, at] + (1.0 - BETA_MOMENT) * g * g
                mom[k, at] = m
                a = g / (jnp.sqrt(m) + EPS_ADAM)
                gf[k, pl.ds(pl.multiple_of(r * band + start, step_rows), step_rows)] = g.astype(jnp.bfloat16)
                return acc + fold(a * a)

            before = jnp.zeros((8, 128), jnp.float32) if h == 0 else nsend[k]
            nsend[k] = lax.fori_loop(0, half // step_rows, one, before)

    class Gather:
        def __init__(self, buf, ss, rs):
            self.buf, self.ss, self.rs = buf, ss, rs

        def copy(self, i, h, k, zz, cc, to):
            at = pl.ds(pl.multiple_of((zz * 2 + cc) * band + h * half, half), half)
            piece = self.buf.at[k, at]
            return remote(piece, piece, self.ss.at[i, h], self.rs.at[i, h], to)

        def got(self, i, h, k, zz, cc, to):
            self.copy(i, h, k, zz, cc, to).wait_recv()

        def start(self, h):
            go(self.copy(0, h, 0, z, c, dev(zm, c)))
            go(self.copy(1, h, 1, z, c, dev(zp, c)))
            go(self.copy(2, h, 1, z, c, dev(zm, c)))
            go(self.copy(3, h, 0, z, c, dev(zp, c)))
            go(self.copy(4, h, 0, z, c, dev(z, sib)))
            go(self.copy(5, h, 1, z, c, dev(z, sib)))

        def forward(self, h):
            self.got(0, h, 0, zp, c, dev(zm, c))
            go(self.copy(6, h, 0, zp, c, dev(zm, c)))
            self.got(1, h, 1, zm, c, dev(zp, c))
            go(self.copy(7, h, 1, zm, c, dev(zp, c)))
            go(self.copy(8, h, 0, zp, c, dev(z, sib)))
            go(self.copy(9, h, 1, zm, c, dev(z, sib)))

        def rest(self, h):
            self.got(2, h, 1, zp, c, dev(zm, c))
            go(self.copy(10, h, 1, zp, c, dev(z, sib)))
            self.got(3, h, 0, zm, c, dev(zp, c))
            go(self.copy(11, h, 0, zm, c, dev(z, sib)))

        def last(self, h):
            self.got(6, h, 0, zf, c, dev(zm, c))
            go(self.copy(12, h, 0, zf, c, dev(z, sib)))
            self.got(7, h, 1, zf, c, dev(zp, c))
            go(self.copy(13, h, 1, zf, c, dev(z, sib)))

        def complete(self):
            for h in (0, 1):
                for i, k, zz in ((4, 0, z), (5, 1, z), (8, 0, zp), (9, 1, zm), (10, 1, zp), (11, 0, zm), (12, 0, zf), (13, 1, zf)):
                    self.got(i, h, k, zz, sib, dev(z, sib))

    gather_g = Gather(gf, gag_ss, gag_rs)
    gather_r = Gather(rf, rag_ss, rag_rs)
    gradient(0)
    gather_g.start(0)
    gradient(1)
    gather_g.start(1)
    mom_cp = pltpu.make_async_copy(mom, moment_out, loc_sem.at[6])
    mom_cp.start()

    left.wait(1)
    left.send(2)
    right.wait(2)
    right.send(3)
    gather_g.forward(0)
    gather_g.forward(1)
    left.wait(2)
    left.send(3)
    gather_g.rest(0)
    gather_g.rest(1)
    right.wait(3)

    def put_right(j, k, value):
        rf[k, pl.ds(pl.multiple_of(r * band + part * j, part), part)] = value

    right.finish(put_right)
    gather_g.last(0)
    gather_g.last(1)
    gather_r.start(0)
    gather_r.start(1)
    gather_g.complete()

    def column(t):
        return pl.ds(pl.multiple_of(((r + 8 + t) % 8) * TILE, TILE), TILE)

    class Outward:
        def __init__(self, held, src, dst, out, xs, xr, ss, rs, x_ss, x_rs):
            self.held, self.src, self.dst, self.out, self.ss, self.rs = held, src, dst, out, ss, rs
            self.xs, self.xr, self.x_ss, self.x_rs = xs, xr, x_ss, x_rs

        def order(self, j):
            return [(j + i) % 4 for i in range(4)]

        def spread(self, stage):
            n = 2 << stage
            for j in range(Q):
                d = self.order(j)
                go(remote(self.held.at[j, pl.ds(0, n)], self.held.at[j, pl.ds(n, n)],
                          self.ss.at[stage, j], self.rs.at[stage, j], across(d[stage])))

        def wait(self, stage):
            n = 2 << stage
            for j in range(Q):
                d = self.order(j)
                dst = self.dst.at[j] if stage == 3 else self.held.at[j, pl.ds(n, n)]
                arrived(dst, self.ss.at[stage, j], self.rs.at[stage, j], across(d[stage]))

        def look(self, j, owner, q):
            d = self.order(j)
            block = ob_ref[owner * NS + q]
            safe = jnp.minimum(block, 31)
            theirs = bits(safe // 2)
            differ = [jnp.where(theirs[t] != mine[t], 1, 0) for t in d]
            entry = 2 * (differ[0] + 2 * differ[1] + 4 * differ[2]) + safe % 2
            return block, differ[3], self.held[j, entry]

        def send(self):
            for j in range(Q):
                d = self.order(j)
                for q in range(NS):
                    self.src[j, q] = self.look(j, shard_at((d[3],)), q)[2]
                go(remote(self.src.at[j], self.dst.at[j], self.ss.at[3, j], self.rs.at[3, j], across(d[3])))

        def finish(self):
            for j in range(Q):
                for q in range(NS):
                    block, far, here = self.look(j, s, q)
                    value = jnp.where(far == 1, self.dst[j, q], here)
                    value = jnp.where(block < 32, value, jnp.zeros_like(value))
                    at = pl.ds(part * j, part)
                    for i, t in enumerate(TILES):
                        piece = value[:, TILE * i:TILE * (i + 1)]
                        self.out[q, at, column(t)] = piece
                        if i in SWAPPED:
                            self.xs[SWAPPED.index(i), q, at] = piece
            for i, t in enumerate(SWAPPED):
                go(remote(self.xs.at[i], self.xr.at[i], self.x_ss.at[i], self.x_rs.at[i], ((r + 8 + TILES[t]) % 8, s)))

        def swap(self):
            for i, t in enumerate(SWAPPED):
                arrived(self.xr.at[i], self.x_ss.at[i], self.x_rs.at[i], ((r + 8 + TILES[t]) % 8, s))
                for q in range(NS):
                    self.out[q, :, column(-TILES[t])] = self.xr[i, q].T

    out_l = Outward(gl_h, gl_s, gl_r, gl_o, gl_xs, gl_xr, glp_ss, glp_rs, xl_ss, xl_rs)
    out_r = Outward(gr_h, gr_s, gr_r, gr_o, gr_xs, gr_xr, grp_ss, grp_rs, xr_ss, xr_rs)

    tile = 256
    mm = functools.partial(lax.dot_general, preferred_element_type=jnp.float32)

    def put_gram(held, k, i, g):
        g = g.astype(jnp.bfloat16)
        for j in range(Q):
            held[j, k, :, pl.ds(TILE * i, TILE)] = g[part * j:part * (j + 1)]

    for k in range(NK):
        band_rows = gf[k, column(0)]
        for i, t in enumerate(TILES):
            put_gram(gl_h, k, i, mm(band_rows, gf[k, column(t)], (((1,), (1,)), ((), ()))))
    out_l.spread(0)
    for k in range(NK):
        band_columns = gf[k, :, column(0)].T
        for i, t in enumerate(TILES):
            put_gram(gr_h, k, i, mm(band_columns, gf[k, :, column(t)], (((1,), (0,)), ((), ()))))
    out_r.spread(0)

    left.wait(3)

    def put_left(j, k, value):
        lh[k, pl.ds(part * j, part)] = value

    left.finish(put_left)

    out_l.wait(0)
    out_l.spread(1)
    out_r.wait(0)
    out_r.spread(1)
    gather_r.forward(0)
    gather_r.forward(1)
    out_l.wait(1)
    out_l.spread(2)
    for h in (0, 1):
        gather_r.rest(h)
        gather_r.last(h)
    out_r.wait(1)
    out_r.spread(2)
    gather_r.complete()

    for k in range(NK):
        @pl.loop(0, width // tile)
        def _(i, k=k):
            at = pl.ds(pl.multiple_of(i * tile, tile), tile)
            tb[at] = mm(gf[k, at], rf[k], (((1,), (0,)), ((), ()))).astype(jnp.bfloat16)

        @pl.loop(0, width // tile)
        def _(i, k=k):
            at = pl.ds(pl.multiple_of(i * tile, tile), tile)
            pv[k, :, at] = mm(lh[k], tb[:, at], (((1,), (0,)), ((), ())))

        def square(i, acc, k=k):
            v = pv[k, pl.ds(pl.multiple_of(i * step_rows, step_rows), step_rows)]
            return acc + fold(v * v)

        nsend[NK + k] = lax.fori_loop(0, band // step_rows, square, jnp.zeros((8, 128), jnp.float32))

    others = [(z, sib, 0)] + [(zz, cc, 1 + 2 * i + cc) for i, zz in enumerate((zm, zp, zf)) for cc in (0, 1)]
    for zz, cc, i in others:
        go(remote(nsend, nrecv.at[r], n_ss.at[i], n_rs.at[r], dev(zz, cc)))
    for zz, cc, i in others:
        src = zz * 2 + cc
        arrived(nrecv.at[src], n_ss.at[i], n_rs.at[src], dev(zz, cc))
    nrecv[r] = nsend[...]
    sums = nrecv[0]
    for i in range(1, 8):
        sums = sums + nrecv[i]
    for k in range(NK):
        adam_total = jnp.sum(sums[k], keepdims=True)
        pre_total = jnp.sum(sums[NK + k], keepdims=True)
        scaling = jnp.sqrt(adam_total) / (jnp.sqrt(pre_total) + EPS_NORM)

        @pl.loop(0, band // step_rows)
        def _(i, k=k, scaling=scaling):
            at = pl.ds(pl.multiple_of(i * step_rows, step_rows), step_rows)
            pv[k, at] = pv[k, at] * scaling

    up_cp = pltpu.make_async_copy(pv, update_out, loc_sem.at[7])
    up_cp.start()

    out_l.wait(2)
    out_l.send()
    out_r.wait(2)
    out_r.send()
    out_l.wait(3)
    out_l.finish()
    out_r.wait(3)
    out_r.finish()
    out_l.swap()
    gl_cp = pltpu.make_async_copy(gl_o, gl_out, loc_sem.at[8])
    gl_cp.start()
    out_r.swap()
    gr_cp = pltpu.make_async_copy(gr_o, gr_out, loc_sem.at[9])
    gr_cp.start()

    for cp in sends:
        cp.wait_send()
    for cp in (mom_cp, up_cp, gl_cp, gr_cp):
        cp.wait()


def body(grads, second_moment, left_stats, right_stats, left_root, right_root, owner_blocks):
    bf16, f32 = jnp.bfloat16, jnp.float32
    band, width = second_moment.shape[1], second_moment.shape[2]
    full = 8 * band
    part = band // Q
    sent = len(TILES) * TILE
    table = owner_blocks.reshape(-1)
    blocks = jnp.arange(32, dtype=jnp.int32)
    inverse = jnp.sum(
        jnp.where(table[None, :] == blocks[:, None], jnp.arange(64, dtype=jnp.int32)[None, :], 0), axis=1
    )
    V, D = pltpu.VMEM, pltpu.SemaphoreType.DMA
    inward = [
        V((NS, band, width), bf16), V((Q, NS, part, width), bf16),
        V((Q, 8, part, width), bf16), V((Q, 8, part, width), bf16),
        V((Q, 4, part, width), bf16), V((Q, 4, part, width), bf16),
        V((Q, 2, part, width), bf16), V((Q, 2, part, width), bf16),
    ]
    outward = [
        V((Q, 16, part, sent), bf16), V((Q, NS, part, sent), bf16),
        V((Q, NS, part, sent), bf16), V((NS, band, width), bf16),
        V((len(SWAPPED), NS, TILE, TILE), bf16), V((len(SWAPPED), NS, TILE, TILE), bf16),
    ]
    scratch = (
        [V((2, band, width), bf16)] * 2
        + [V((band, width), bf16)] * 2
        + [V((2, band, width), bf16)] * 2
        + [V((2, band, width), bf16)]
        + [V((band, width), f32)] * 4
        + [V((band, width), bf16)] * 2
        + [V((2, band, width), bf16)]
        + [V((2, band, width), f32)] * 2
        + [V((2, full, width), bf16)] * 2
        + [V((full, width), bf16)]
        + [V((2, band, width), f32)]
        + [V((2, band, width), bf16)]
        + [V((4, 8, 128), f32), V((8, 4, 8, 128), f32)]
        + inward + inward + outward + outward
        + [D((10,)), D((8, 2)), D((8, 2))] + [D((14, 2))] * 4
        + [D((4, Q))] * 8
        + [D((len(SWAPPED),))] * 4
        + [D((7,)), D((8,))]
    )
    hbm = pl.BlockSpec(memory_space=pl.ANY)
    smem = pl.BlockSpec(memory_space=pltpu.SMEM)
    update, moment_new, gram_left, gram_right = pl.pallas_call(
        kernel,
        out_shape=(
            jax.ShapeDtypeStruct((2, band, width), f32),
            jax.ShapeDtypeStruct((2, band, width), f32),
            jax.ShapeDtypeStruct((NS, band, width), bf16),
            jax.ShapeDtypeStruct((NS, band, width), bf16),
        ),
        in_specs=[smem, smem, hbm, hbm, hbm, hbm],
        out_specs=(hbm, hbm, hbm, hbm),
        scratch_shapes=scratch,
        compiler_params=pltpu.CompilerParams(
            collective_id=0, has_side_effects=True, vmem_limit_bytes=60 * 2**20
        ),
        name="shampoo",
    )(table, inverse, grads, second_moment, left_root, right_root)
    left_new = BETA_STAT * left_stats + (1.0 - BETA_STAT) * gram_left.astype(f32)
    right_new = BETA_STAT * right_stats + (1.0 - BETA_STAT) * gram_right.astype(f32)
    return (update, moment_new, left_new, right_new)


def solution(mesh):
    in_specs = (
        P("replica", "shard", None, None),
        P("shard", "replica", None),
        P("shard", "replica", None),
        P("shard", "replica", None),
        P("shard", "replica", None),
        P("shard", "replica", None),
        P(),
    )
    out_specs = (
        P("shard", "replica", None),
        P("shard", "replica", None),
        P("shard", "replica", None),
        P("shard", "replica", None),
    )
    return jax.shard_map(body, mesh=mesh, in_specs=in_specs, out_specs=out_specs, check_vma=False)
```

```python
import functools

import jax
import jax.numpy as jnp
from jax import lax
from jax.experimental import pallas as pl
from jax.experimental.pallas import tpu as pltpu
from jax.sharding import PartitionSpec as P

BETA_STAT = 0.99
BETA_MOMENT = 0.95
EPS_ADAM = 1e-08
EPS_NORM = 1e-06
MESH = pl.DeviceIdType.MESH

NS = 4
NK = 2
Q = 4
TILES = (0, 1, -2, 3, 4)
SWAPPED = (1, 2, 3)
TILE = 128


def flip(v, low, high):
    if low:
        v = v + 1 - 2 * (v % 2)
    if high:
        v = 3 - v
    return v


def gray_bits(v):
    return ((v + 1) // 2) % 2, v // 2


def kernel(
    ob_ref, inv_ref, grads, sm_hbm, lroot, rroot,
    update_out, moment_out, gl_out, gr_out,
    far0, far1, sm0, sm1, nr0, nr1, so, mg0, mg1, ms0, ms1, own0, own1, ownb,
    smv, mom, gf, rf, tb, pv, lh, nsend, nrecv,
    r_own, r_v0, r_sa, r_ra, r_sb, r_rb, r_sc, r_rc,
    l_own, l_v0, l_sa, l_ra, l_sb, l_rb, l_sc, l_rc,
    gl_h, gl_s, gl_r, gl_o, gl_xs, gl_xr, gr_h, gr_s, gr_r, gr_o, gr_xs, gr_xr,
    loc_sem, a_ss, a_rs, gag_ss, gag_rs, rag_ss, rag_rs,
    rp_ss, rp_rs, lp_ss, lp_rs, glp_ss, glp_rs, grp_ss, grp_rs, xl_ss, xl_rs, xr_ss, xr_rs, n_ss, n_rs,
):
    band = sm_hbm.shape[1]
    width = sm_hbm.shape[2]
    part = band // Q
    r = lax.axis_index("replica")
    s = lax.axis_index("shard")
    z, c = r // 2, r % 2
    x, y = s // 4, s % 4
    zp, zm, zf = (z + 1) % 4, (z + 3) % 4, (z + 2) % 4
    sib = 1 - c

    def dev(zz, cc):
        return (zz * 2 + cc, s)

    def rows(zz, cc):
        return pl.ds((zz * 2 + cc) * band, band)

    half = band // 2

    def half_rows(zz, cc, h):
        return pl.ds(pl.multiple_of((zz * 2 + cc) * band + h * half, half), half)

    def shard_at(flips):
        return 4 * flip(x, 2 in flips, 3 in flips) + flip(y, 0 in flips, 1 in flips)

    def across(dim):
        return (r, shard_at((dim,)))

    def bits(shard):
        ya, yb = gray_bits(shard % 4)
        xa, xb = gray_bits(shard // 4)
        return (ya, yb, xa, xb)

    mine = bits(s)

    def remote(src, dst, ss, rs, to):
        return pltpu.make_async_remote_copy(
            src_ref=src, dst_ref=dst, send_sem=ss, recv_sem=rs, device_id=to, device_id_type=MESH
        )

    me = (r, s)

    def arrived(dst, ss, rs, to):
        remote(dst, dst, ss, rs, to).wait_recv()

    sends = []

    def go(cp):
        cp.start()
        sends.append(cp)

    locs = [
        pltpu.make_async_copy(grads.at[0, :, half_rows(zm, c, 0)], own0, loc_sem.at[0]),
        pltpu.make_async_copy(grads.at[0, :, half_rows(zp, c, 1)], own1, loc_sem.at[1]),
        pltpu.make_async_copy(grads.at[0, :, rows(z, c)], ownb, loc_sem.at[2]),
        pltpu.make_async_copy(sm_hbm, smv, loc_sem.at[3]),
        pltpu.make_async_copy(rroot, r_own, loc_sem.at[4]),
        pltpu.make_async_copy(lroot, l_own, loc_sem.at[5]),
    ]
    for cp in locs:
        cp.start()

    barrier = pltpu.get_barrier_semaphore()
    partners = [dev(z, sib)] + [dev(zz, cc) for zz in (zm, zp, zf) for cc in (0, 1)]
    partners += [across(d) for d in range(4)]
    for p in partners:
        pl.semaphore_signal(barrier, inc=1, device_id=p, device_id_type=MESH)
    pl.semaphore_wait(barrier, len(partners))

    def far_send(k):
        for j in (0, 1):
            go(remote(grads.at[0, k, half_rows(zf, j, 0)], far0.at[k, c], a_ss.at[k, 0, j], a_rs.at[k, 0, c], dev(zm, j)))
            go(remote(grads.at[0, k, half_rows(zf, j, 1)], far1.at[k, c], a_ss.at[k, 1, j], a_rs.at[k, 1, c], dev(zp, j)))

    def side_send(k):
        go(remote(grads.at[0, k, half_rows(zm, sib, 0)], sm0.at[k], a_ss.at[k, 2, 0], a_rs.at[k, 2, 0], dev(z, sib)))
        go(remote(grads.at[0, k, half_rows(zp, sib, 1)], sm1.at[k], a_ss.at[k, 2, 1], a_rs.at[k, 2, 1], dev(z, sib)))
        go(remote(grads.at[0, k, rows(z, sib)], so.at[k], a_ss.at[k, 3, 0], a_rs.at[k, 3, 0], dev(z, sib)))

    def near_send(k, j):
        there = (c, sib)[j]
        go(remote(grads.at[0, k, half_rows(zm, there, 1)], nr1.at[k, c], a_ss.at[k, 4, j], a_rs.at[k, 4, c], dev(zm, there)))
        go(remote(grads.at[0, k, half_rows(zp, there, 0)], nr0.at[k, c], a_ss.at[k, 5, j], a_rs.at[k, 5, c], dev(zp, there)))

    step_rows = 16

    def f32(v):
        return v.astype(jnp.float32)

    def far_wait(k):
        for cc in (0, 1):
            arrived(far0.at[k, cc], a_ss.at[k, 0, cc], a_rs.at[k, 0, cc], dev(zm, cc))
            arrived(far1.at[k, cc], a_ss.at[k, 1, cc], a_rs.at[k, 1, cc], dev(zp, cc))
        arrived(sm0.at[k], a_ss.at[k, 2, 0], a_rs.at[k, 2, 0], dev(z, sib))
        arrived(sm1.at[k], a_ss.at[k, 2, 1], a_rs.at[k, 2, 1], dev(z, sib))

    def merge(k):
        @pl.loop(0, half // step_rows)
        def _(i):
            at = pl.ds(pl.multiple_of(i * step_rows, step_rows), step_rows)
            ms0[k, at] = (f32(own0[k, at]) + f32(sm0[k, at])) + (f32(far0[k, 0, at]) + f32(far0[k, 1, at]))
            ms1[k, at] = (f32(own1[k, at]) + f32(sm1[k, at])) + (f32(far1[k, 0, at]) + f32(far1[k, 1, at]))

        go(remote(ms0.at[k], mg0.at[k], a_ss.at[k, 6, 0], a_rs.at[k, 6, 0], dev(zm, c)))
        go(remote(ms1.at[k], mg1.at[k], a_ss.at[k, 6, 1], a_rs.at[k, 6, 1], dev(zp, c)))

    def fold(v):
        v = v[:8] + v[8:]
        total = v[:, :128]
        for i in range(1, width // 128):
            total = total + v[:, 128 * i:128 * (i + 1)]
        return total

    def gradient(k):
        for cc in (0, 1):
            arrived(nr1.at[k, cc], a_ss.at[k, 4, cc], a_rs.at[k, 4, cc], dev(zm, cc))
            arrived(nr0.at[k, cc], a_ss.at[k, 5, cc], a_rs.at[k, 5, cc], dev(zp, cc))
        arrived(so.at[k], a_ss.at[k, 3, 0], a_rs.at[k, 3, 0], dev(z, sib))
        arrived(mg0.at[k], a_ss.at[k, 6, 0], a_rs.at[k, 6, 0], dev(zm, c))
        arrived(mg1.at[k], a_ss.at[k, 6, 1], a_rs.at[k, 6, 1], dev(zp, c))
        acc = jnp.zeros((8, 128), jnp.float32)
        for h, near, merged in ((0, nr0, mg0), (1, nr1, mg1)):
            def one(i, acc, h=h, near=near, merged=merged):
                inner = pl.ds(pl.multiple_of(i * step_rows, step_rows), step_rows)
                start = pl.multiple_of(h * half + i * step_rows, step_rows)
                at = pl.ds(start, step_rows)
                g = (f32(ownb[k, at]) + f32(so[k, at])) + (f32(near[k, 0, inner]) + f32(near[k, 1, inner])) + merged[k, inner]
                m = BETA_MOMENT * smv[k, at] + (1.0 - BETA_MOMENT) * g * g
                mom[k, at] = m
                a = g / (jnp.sqrt(m) + EPS_ADAM)
                gf[k, pl.ds(pl.multiple_of(r * band + start, step_rows), step_rows)] = g.astype(jnp.bfloat16)
                return acc + fold(a * a)

            acc = lax.fori_loop(0, half // step_rows, one, acc)
        nsend[k] = acc

    class Inward:
        def __init__(self, root, own, v0, sa, ra, sb, rb, sc, rc, ss, rs):
            self.root, self.own, self.v0 = root, own, v0
            self.bufs = [(sa, ra), (sb, rb), (sc, rc)]
            self.ss, self.rs = ss, rs

        def order(self, j):
            return [(j + i) % 4 for i in range(4)]

        def start(self):
            for j in range(Q):
                d = self.order(j)
                go(remote(self.root.at[:, pl.ds(part * j, part)], self.v0.at[j],
                          self.ss.at[0, j], self.rs.at[0, j], across(d[3])))

        def wait(self, stage):
            for j in range(Q):
                d = self.order(j)
                dst = self.v0.at[j] if stage == 0 else self.bufs[stage - 1][1].at[j]
                arrived(dst, self.ss.at[stage, j], self.rs.at[stage, j], across(d[3 - stage]))

        def pick(self, j, level, home_flips, k, ea, eb):
            d = self.order(j)
            place = inv_ref[2 * shard_at(home_flips) + k]
            owner, slot = place // NS, place % NS
            theirs = bits(owner)
            value = jnp.where(theirs[d[3]] != mine[d[3]], self.v0[j, slot],
                              self.own[slot, pl.ds(part * j, part)])
            if level >= 1:
                value = jnp.where(theirs[d[2]] != mine[d[2]], self.bufs[0][1][j, ea], value)
            if level >= 2:
                value = jnp.where(theirs[d[1]] != mine[d[1]], self.bufs[1][1][j, eb], value)
            if level >= 3:
                value = jnp.where(theirs[d[0]] != mine[d[0]], self.bufs[2][1][j, k], value)
            return value

        def send(self, stage):
            src, dst = self.bufs[stage - 1]
            for j in range(Q):
                d = self.order(j)
                for e in range(8 >> (stage - 1)):
                    k, r0, r1 = e % 2, (e // 2) % 2, e // 4
                    if stage == 1:
                        flips = (d[2],) + ((d[0],) if r0 else ()) + ((d[1],) if r1 else ())
                        ea = eb = None
                    elif stage == 2:
                        flips = (d[1],) + ((d[0],) if r0 else ())
                        ea, eb = 4 + 2 * r0 + k, None
                    else:
                        flips = (d[0],)
                        ea, eb = 2 + k, 2 + k
                    src[j, e] = self.pick(j, stage - 1, flips, k, ea, eb)
                go(remote(src.at[j], dst.at[j], self.ss.at[stage, j], self.rs.at[stage, j], across(d[3 - stage])))

        def finish(self, put):
            for j in range(Q):
                for k in range(NK):
                    put(j, k, self.pick(j, 3, (), k, k, k))

    right = Inward(rroot, r_own, r_v0, r_sa, r_ra, r_sb, r_rb, r_sc, r_rc, rp_ss, rp_rs)
    left = Inward(lroot, l_own, l_v0, l_sa, l_ra, l_sb, l_rb, l_sc, l_rc, lp_ss, lp_rs)
    class Gather:
        def __init__(self, buf, ss, rs):
            self.buf, self.ss, self.rs = buf, ss, rs

        def copy(self, i, k, h, zz, cc, to):
            piece = self.buf.at[k, half_rows(zz, cc, h)]
            return remote(piece, piece, self.ss.at[i, k], self.rs.at[i, k], to)

        def got(self, i, k, h, zz, cc, to):
            self.copy(i, k, h, zz, cc, to).wait_recv()

        def start(self, k):
            go(self.copy(0, k, 0, z, c, dev(zm, c)))
            go(self.copy(1, k, 1, z, c, dev(zp, c)))
            go(self.copy(2, k, 1, z, c, dev(zm, c)))
            go(self.copy(3, k, 0, z, c, dev(zp, c)))
            go(self.copy(4, k, 0, z, c, dev(z, sib)))
            go(self.copy(5, k, 1, z, c, dev(z, sib)))

        def forward(self, k):
            self.got(0, k, 0, zp, c, dev(zm, c))
            go(self.copy(6, k, 0, zp, c, dev(zm, c)))
            self.got(1, k, 1, zm, c, dev(zp, c))
            go(self.copy(7, k, 1, zm, c, dev(zp, c)))
            go(self.copy(8, k, 0, zp, c, dev(z, sib)))
            go(self.copy(9, k, 1, zm, c, dev(z, sib)))

        def rest(self, k):
            self.got(2, k, 1, zp, c, dev(zm, c))
            go(self.copy(10, k, 1, zp, c, dev(z, sib)))
            self.got(3, k, 0, zm, c, dev(zp, c))
            go(self.copy(11, k, 0, zm, c, dev(z, sib)))

        def last(self, k):
            self.got(6, k, 0, zf, c, dev(zm, c))
            go(self.copy(12, k, 0, zf, c, dev(z, sib)))
            self.got(7, k, 1, zf, c, dev(zp, c))
            go(self.copy(13, k, 1, zf, c, dev(z, sib)))

        def complete(self, k):
            for i, h, zz in ((4, 0, z), (5, 1, z), (8, 0, zp), (9, 1, zm), (10, 1, zp), (11, 0, zm), (12, 0, zf), (13, 1, zf)):
                self.got(i, k, h, zz, sib, dev(z, sib))

    gather_g = Gather(gf, gag_ss, gag_rs)
    gather_r = Gather(rf, rag_ss, rag_rs)

    def put_right(j, k, value):
        rf[k, pl.ds(pl.multiple_of(r * band + part * j, part), part)] = value

    def put_left(j, k, value):
        lh[k, pl.ds(part * j, part)] = value

    def column(t):
        return pl.ds(pl.multiple_of(((r + 8 + t) % 8) * TILE, TILE), TILE)

    class Outward:
        def __init__(self, held, src, dst, out, xs, xr, ss, rs, x_ss, x_rs):
            self.held, self.src, self.dst, self.out, self.ss, self.rs = held, src, dst, out, ss, rs
            self.xs, self.xr, self.x_ss, self.x_rs = xs, xr, x_ss, x_rs

        def order(self, j):
            return [(j + i) % 4 for i in range(4)]

        def spread(self, k, stage):
            n = 1 << stage
            for j in range(Q):
                d = self.order(j)
                go(remote(self.held.at[j, k, pl.ds(0, n)], self.held.at[j, k, pl.ds(n, n)],
                          self.ss.at[3 * k + stage, j], self.rs.at[3 * k + stage, j], across(d[stage])))

        def wait(self, k, stage):
            n = 1 << stage
            for j in range(Q):
                d = self.order(j)
                arrived(self.held.at[j, k, pl.ds(n, n)], self.ss.at[3 * k + stage, j], self.rs.at[3 * k + stage, j], across(d[stage]))

        def wait_last(self):
            for j in range(Q):
                d = self.order(j)
                arrived(self.dst.at[j], self.ss.at[6, j], self.rs.at[6, j], across(d[3]))

        def look(self, j, owner, q):
            d = self.order(j)
            block = ob_ref[owner * NS + q]
            safe = jnp.minimum(block, 31)
            theirs = bits(safe // 2)
            differ = [jnp.where(theirs[t] != mine[t], 1, 0) for t in d]
            return block, differ[3], self.held[j, safe % 2, differ[0] + 2 * differ[1] + 4 * differ[2]]

        def send(self):
            for j in range(Q):
                d = self.order(j)
                for q in range(NS):
                    self.src[j, q] = self.look(j, shard_at((d[3],)), q)[2]
                go(remote(self.src.at[j], self.dst.at[j], self.ss.at[6, j], self.rs.at[6, j], across(d[3])))

        def finish(self):
            for j in range(Q):
                for q in range(NS):
                    block, far, here = self.look(j, s, q)
                    value = jnp.where(far == 1, self.dst[j, q], here)
                    value = jnp.where(block < 32, value, jnp.zeros_like(value))
                    at = pl.ds(part * j, part)
                    for i, t in enumerate(TILES):
                        piece = value[:, TILE * i:TILE * (i + 1)]
                        self.out[q, at, column(t)] = piece
                        if i in SWAPPED:
                            self.xs[SWAPPED.index(i), q, at] = piece
            for i, t in enumerate(SWAPPED):
                go(remote(self.xs.at[i], self.xr.at[i], self.x_ss.at[i], self.x_rs.at[i], ((r + 8 + TILES[t]) % 8, s)))

        def swap(self):
            for i, t in enumerate(SWAPPED):
                arrived(self.xr.at[i], self.x_ss.at[i], self.x_rs.at[i], ((r + 8 + TILES[t]) % 8, s))
                for q in range(NS):
                    self.out[q, :, column(-TILES[t])] = self.xr[i, q].T

    out_l = Outward(gl_h, gl_s, gl_r, gl_o, gl_xs, gl_xr, glp_ss, glp_rs, xl_ss, xl_rs)
    out_r = Outward(gr_h, gr_s, gr_r, gr_o, gr_xs, gr_xr, grp_ss, grp_rs, xr_ss, xr_rs)

    tile = 256
    mm = functools.partial(lax.dot_general, preferred_element_type=jnp.float32)

    def put_gram(held, k, i, g):
        g = g.astype(jnp.bfloat16)
        for j in range(Q):
            held[j, k, 0, :, pl.ds(TILE * i, TILE)] = g[part * j:part * (j + 1)]

    def gram_left(k):
        band_rows = gf[k, column(0)]
        for i, t in enumerate(TILES):
            put_gram(gl_h, k, i, mm(band_rows, gf[k, column(t)], (((1,), (1,)), ((), ()))))

    def gram_right(k):
        band_columns = gf[k, :, column(0)].T
        for i, t in enumerate(TILES):
            put_gram(gr_h, k, i, mm(band_columns, gf[k, :, column(t)], (((1,), (0,)), ((), ()))))

    def precondition(k):
        @pl.loop(0, width // tile)
        def _(i):
            at = pl.ds(pl.multiple_of(i * tile, tile), tile)
            tb[at] = mm(gf[k, at], rf[k], (((1,), (0,)), ((), ()))).astype(jnp.bfloat16)

        @pl.loop(0, width // tile)
        def _(i):
            at = pl.ds(pl.multiple_of(i * tile, tile), tile)
            pv[k, :, at] = mm(lh[k], tb[:, at], (((1,), (0,)), ((), ())))

        def square(i, acc):
            v = pv[k, pl.ds(pl.multiple_of(i * step_rows, step_rows), step_rows)]
            return acc + fold(v * v)

        nsend[NK + k] = lax.fori_loop(0, band // step_rows, square, jnp.zeros((8, 128), jnp.float32))

    others = [(z, sib, 0)] + [(zz, cc, 1 + 2 * i + cc) for i, zz in enumerate((zm, zp, zf)) for cc in (0, 1)]

    def norms_send():
        for zz, cc, i in others:
            go(remote(nsend, nrecv.at[r], n_ss.at[i], n_rs.at[r], dev(zz, cc)))

    def norms_apply():
        for zz, cc, i in others:
            src = zz * 2 + cc
            arrived(nrecv.at[src], n_ss.at[i], n_rs.at[src], dev(zz, cc))
        nrecv[r] = nsend[...]
        sums = nrecv[0]
        for i in range(1, 8):
            sums = sums + nrecv[i]
        for k in range(NK):
            adam_total = jnp.sum(sums[k], keepdims=True)
            pre_total = jnp.sum(sums[NK + k], keepdims=True)
            scaling = jnp.sqrt(adam_total) / (jnp.sqrt(pre_total) + EPS_NORM)

            @pl.loop(0, band // step_rows)
            def _(i, k=k, scaling=scaling):
                at = pl.ds(pl.multiple_of(i * step_rows, step_rows), step_rows)
                pv[k, at] = pv[k, at] * scaling

    mom_cp = pltpu.make_async_copy(mom, moment_out, loc_sem.at[6])
    up_cp = pltpu.make_async_copy(pv, update_out, loc_sem.at[7])
    gl_cp = pltpu.make_async_copy(gl_o, gl_out, loc_sem.at[8])
    gr_cp = pltpu.make_async_copy(gr_o, gr_out, loc_sem.at[9])

    far_send(0)
    side_send(0)
    near_send(0, 0)
    right.start()
    side_send(1)
    locs[0].wait()
    locs[1].wait()
    locs[4].wait()
    right.wait(0)
    right.send(1)
    left.start()
    far_wait(0)
    near_send(0, 1)
    merge(0)
    far_send(1)
    locs[5].wait()
    locs[2].wait()
    locs[3].wait()
    gradient(0)
    gather_g.start(0)
    near_send(1, 0)
    left.wait(0)
    left.send(1)
    right.wait(1)
    right.send(2)
    far_wait(1)
    merge(1)
    gather_g.forward(0)
    near_send(1, 1)
    gather_g.rest(0)
    gather_g.last(0)
    gather_g.complete(0)
    gram_left(0)
    out_l.spread(0, 0)
    gram_right(0)
    out_r.spread(0, 0)
    right.wait(2)
    right.send(3)
    out_l.wait(0, 0)
    out_l.spread(0, 1)
    out_r.wait(0, 0)
    out_r.spread(0, 1)
    gradient(1)
    gather_g.start(1)
    mom_cp.start()
    left.wait(1)
    left.send(2)
    right.wait(3)
    right.finish(put_right)
    gather_g.forward(1)
    gather_r.start(0)
    gather_g.rest(1)
    out_l.wait(0, 1)
    out_l.spread(0, 2)
    out_r.wait(0, 1)
    out_r.spread(0, 2)
    gather_g.last(1)
    gather_r.start(1)
    gather_g.complete(1)
    gram_left(1)
    out_l.spread(1, 0)
    gram_right(1)
    out_r.spread(1, 0)
    left.wait(2)
    left.send(3)
    gather_r.forward(0)
    out_l.wait(1, 0)
    out_l.spread(1, 1)
    out_r.wait(1, 0)
    out_r.spread(1, 1)
    gather_r.forward(1)
    gather_r.rest(0)
    gather_r.last(0)
    left.wait(3)
    left.finish(put_left)
    out_l.wait(1, 1)
    out_l.spread(1, 2)
    out_r.wait(1, 1)
    out_r.spread(1, 2)
    gather_r.rest(1)
    gather_r.last(1)
    gather_r.complete(0)
    precondition(0)
    out_l.wait(0, 2)
    out_r.wait(0, 2)
    out_l.wait(1, 2)
    out_l.send()
    out_r.wait(1, 2)
    out_r.send()
    gather_r.complete(1)
    precondition(1)
    norms_send()
    out_l.wait_last()
    out_l.finish()
    out_r.wait_last()
    out_r.finish()
    norms_apply()
    up_cp.start()
    out_l.swap()
    gl_cp.start()
    out_r.swap()
    gr_cp.start()

    for cp in sends:
        cp.wait_send()
    for cp in (mom_cp, up_cp, gl_cp, gr_cp):
        cp.wait()


def body(grads, second_moment, left_stats, right_stats, left_root, right_root, owner_blocks):
    bf16, f32 = jnp.bfloat16, jnp.float32
    band, width = second_moment.shape[1], second_moment.shape[2]
    full = 8 * band
    part = band // Q
    half = band // 2
    sent = len(TILES) * TILE
    table = owner_blocks.reshape(-1)
    blocks = jnp.arange(32, dtype=jnp.int32)
    inverse = jnp.sum(
        jnp.where(table[None, :] == blocks[:, None], jnp.arange(64, dtype=jnp.int32)[None, :], 0), axis=1
    )
    V, D = pltpu.VMEM, pltpu.SemaphoreType.DMA
    inward = [
        V((NS, band, width), bf16), V((Q, NS, part, width), bf16),
        V((Q, 8, part, width), bf16), V((Q, 8, part, width), bf16),
        V((Q, 4, part, width), bf16), V((Q, 4, part, width), bf16),
        V((Q, 2, part, width), bf16), V((Q, 2, part, width), bf16),
    ]
    outward = [
        V((Q, NK, 8, part, sent), bf16), V((Q, NS, part, sent), bf16),
        V((Q, NS, part, sent), bf16), V((NS, band, width), bf16),
        V((len(SWAPPED), NS, TILE, TILE), bf16), V((len(SWAPPED), NS, TILE, TILE), bf16),
    ]
    scratch = (
        [V((NK, 2, half, width), bf16)] * 2
        + [V((NK, half, width), bf16)] * 2
        + [V((NK, 2, half, width), bf16)] * 2
        + [V((NK, band, width), bf16)]
        + [V((NK, half, width), f32)] * 4
        + [V((NK, half, width), bf16)] * 2
        + [V((NK, band, width), bf16)]
        + [V((2, band, width), f32)] * 2
        + [V((2, full, width), bf16)] * 2
        + [V((full, width), bf16)]
        + [V((2, band, width), f32)]
        + [V((2, band, width), bf16)]
        + [V((4, 8, 128), f32), V((8, 4, 8, 128), f32)]
        + inward + inward + outward + outward
        + [D((10,)), D((NK, 7, 2)), D((NK, 7, 2))] + [D((14, 2))] * 4
        + [D((4, Q))] * 4
        + [D((7, Q))] * 4
        + [D((len(SWAPPED),))] * 4
        + [D((7,)), D((8,))]
    )
    hbm = pl.BlockSpec(memory_space=pl.ANY)
    smem = pl.BlockSpec(memory_space=pltpu.SMEM)
    update, moment_new, gram_left, gram_right = pl.pallas_call(
        kernel,
        out_shape=(
            jax.ShapeDtypeStruct((2, band, width), f32),
            jax.ShapeDtypeStruct((2, band, width), f32),
            jax.ShapeDtypeStruct((NS, band, width), bf16),
            jax.ShapeDtypeStruct((NS, band, width), bf16),
        ),
        in_specs=[smem, smem, hbm, hbm, hbm, hbm],
        out_specs=(hbm, hbm, hbm, hbm),
        scratch_shapes=scratch,
        compiler_params=pltpu.CompilerParams(
            collective_id=0, has_side_effects=True, vmem_limit_bytes=50 * 2**20
        ),
        name="shampoo",
    )(table, inverse, grads, second_moment, left_root, right_root)
    left_new = BETA_STAT * left_stats + (1.0 - BETA_STAT) * gram_left.astype(f32)
    right_new = BETA_STAT * right_stats + (1.0 - BETA_STAT) * gram_right.astype(f32)
    return (update, moment_new, left_new, right_new)


def solution(mesh):
    in_specs = (
        P("replica", "shard", None, None),
        P("shard", "replica", None),
        P("shard", "replica", None),
        P("shard", "replica", None),
        P("shard", "replica", None),
        P("shard", "replica", None),
        P(),
    )
    out_specs = (
        P("shard", "replica", None),
        P("shard", "replica", None),
        P("shard", "replica", None),
        P("shard", "replica", None),
    )
    return jax.shard_map(body, mesh=mesh, in_specs=in_specs, out_specs=out_specs, check_vma=False)
```

```python
import functools

import jax
import jax.numpy as jnp
from jax import lax
from jax.experimental import pallas as pl
from jax.experimental.pallas import tpu as pltpu
from jax.sharding import PartitionSpec as P

BETA_STAT = 0.99
BETA_MOMENT = 0.95
EPS_ADAM = 1e-08
EPS_NORM = 1e-06
MESH = pl.DeviceIdType.MESH

NS = 4
NK = 2
Q = 4
TILES = (0, 1, -2, 3, 4)
SWAPPED = (1, 2, 3)
TILE = 128


def flip(v, low, high):
    if low:
        v = v + 1 - 2 * (v % 2)
    if high:
        v = 3 - v
    return v


def gray_bits(v):
    return ((v + 1) // 2) % 2, v // 2


def kernel(
    ob_ref, inv_ref, grads, sm_hbm, lroot, rroot,
    update_out, moment_out, gl_out, gr_out,
    far0, far1, sm0, sm1, nr0, nr1, so, mg0, mg1, ms0, ms1, own0, own1, ownb,
    smv, mom, gf, rf, tb, pv, lh, nsend, nrecv,
    r_own, r_v0, r_sa, r_ra, r_sb, r_rb, r_sc, r_rc,
    l_own, l_v0, l_sa, l_ra, l_sb, l_rb, l_sc, l_rc,
    gl_h, gl_s, gl_r, gl_o, gl_xs, gl_xr, gr_h, gr_s, gr_r, gr_o, gr_xs, gr_xr,
    loc_sem, a_ss, a_rs, gag_ss, gag_rs, rag_ss, rag_rs,
    rp_ss, rp_rs, lp_ss, lp_rs, glp_ss, glp_rs, grp_ss, grp_rs, xl_ss, xl_rs, xr_ss, xr_rs, n_ss, n_rs,
):
    band = sm_hbm.shape[1]
    width = sm_hbm.shape[2]
    part = band // Q
    r = lax.axis_index("replica")
    s = lax.axis_index("shard")
    z, c = r // 2, r % 2
    x, y = s // 4, s % 4
    zp, zm, zf = (z + 1) % 4, (z + 3) % 4, (z + 2) % 4
    sib = 1 - c

    def dev(zz, cc):
        return (zz * 2 + cc, s)

    def rows(zz, cc):
        return pl.ds((zz * 2 + cc) * band, band)

    half = band // 2

    def half_rows(zz, cc, h):
        return pl.ds(pl.multiple_of((zz * 2 + cc) * band + h * half, half), half)

    def shard_at(flips):
        return 4 * flip(x, 2 in flips, 3 in flips) + flip(y, 0 in flips, 1 in flips)

    def across(dim):
        return (r, shard_at((dim,)))

    def bits(shard):
        ya, yb = gray_bits(shard % 4)
        xa, xb = gray_bits(shard // 4)
        return (ya, yb, xa, xb)

    mine = bits(s)

    def remote(src, dst, ss, rs, to):
        return pltpu.make_async_remote_copy(
            src_ref=src, dst_ref=dst, send_sem=ss, recv_sem=rs, device_id=to, device_id_type=MESH
        )

    me = (r, s)

    def arrived(dst, ss, rs, to):
        remote(dst, dst, ss, rs, to).wait_recv()

    sends = []

    def go(cp):
        cp.start()
        sends.append(cp)

    locs = [
        pltpu.make_async_copy(grads.at[0, :, half_rows(zm, c, 0)], own0, loc_sem.at[0]),
        pltpu.make_async_copy(grads.at[0, :, half_rows(zp, c, 1)], own1, loc_sem.at[1]),
        pltpu.make_async_copy(grads.at[0, :, rows(z, c)], ownb, loc_sem.at[2]),
        pltpu.make_async_copy(sm_hbm, smv, loc_sem.at[3]),
        pltpu.make_async_copy(rroot, r_own, loc_sem.at[4]),
        pltpu.make_async_copy(lroot, l_own, loc_sem.at[5]),
    ]
    for cp in locs:
        cp.start()

    barrier = pltpu.get_barrier_semaphore()
    partners = [dev(z, sib)] + [dev(zz, cc) for zz in (zm, zp, zf) for cc in (0, 1)]
    partners += [across(d) for d in range(4)]
    for p in partners:
        pl.semaphore_signal(barrier, inc=1, device_id=p, device_id_type=MESH)
    pl.semaphore_wait(barrier, len(partners))

    def far_send(k):
        for j in (0, 1):
            go(remote(grads.at[0, k, half_rows(zf, j, 0)], far0.at[k, c], a_ss.at[k, 0, j], a_rs.at[k, 0, c], dev(zm, j)))
            go(remote(grads.at[0, k, half_rows(zf, j, 1)], far1.at[k, c], a_ss.at[k, 1, j], a_rs.at[k, 1, c], dev(zp, j)))

    def side_send(k):
        go(remote(grads.at[0, k, half_rows(zm, sib, 0)], sm0.at[k], a_ss.at[k, 2, 0], a_rs.at[k, 2, 0], dev(z, sib)))
        go(remote(grads.at[0, k, half_rows(zp, sib, 1)], sm1.at[k], a_ss.at[k, 2, 1], a_rs.at[k, 2, 1], dev(z, sib)))
        go(remote(grads.at[0, k, rows(z, sib)], so.at[k], a_ss.at[k, 3, 0], a_rs.at[k, 3, 0], dev(z, sib)))

    def near_send(k, j):
        there = (c, sib)[j]
        go(remote(grads.at[0, k, half_rows(zm, there, 1)], nr1.at[k, c], a_ss.at[k, 4, j], a_rs.at[k, 4, c], dev(zm, there)))
        go(remote(grads.at[0, k, half_rows(zp, there, 0)], nr0.at[k, c], a_ss.at[k, 5, j], a_rs.at[k, 5, c], dev(zp, there)))

    step_rows = 16

    def f32(v):
        return v.astype(jnp.float32)

    def far_wait(k):
        for cc in (0, 1):
            arrived(far0.at[k, cc], a_ss.at[k, 0, cc], a_rs.at[k, 0, cc], dev(zm, cc))
            arrived(far1.at[k, cc], a_ss.at[k, 1, cc], a_rs.at[k, 1, cc], dev(zp, cc))
        arrived(sm0.at[k], a_ss.at[k, 2, 0], a_rs.at[k, 2, 0], dev(z, sib))
        arrived(sm1.at[k], a_ss.at[k, 2, 1], a_rs.at[k, 2, 1], dev(z, sib))

    def merge(k):
        @pl.loop(0, half // step_rows)
        def _(i):
            at = pl.ds(pl.multiple_of(i * step_rows, step_rows), step_rows)
            ms0[k, at] = (f32(own0[k, at]) + f32(sm0[k, at])) + (f32(far0[k, 0, at]) + f32(far0[k, 1, at]))
            ms1[k, at] = (f32(own1[k, at]) + f32(sm1[k, at])) + (f32(far1[k, 0, at]) + f32(far1[k, 1, at]))

        go(remote(ms0.at[k], mg0.at[k], a_ss.at[k, 6, 0], a_rs.at[k, 6, 0], dev(zm, c)))
        go(remote(ms1.at[k], mg1.at[k], a_ss.at[k, 6, 1], a_rs.at[k, 6, 1], dev(zp, c)))

    def fold(v):
        v = v[:8] + v[8:]
        total = v[:, :128]
        for i in range(1, width // 128):
            total = total + v[:, 128 * i:128 * (i + 1)]
        return total

    def gradient(k):
        for cc in (0, 1):
            arrived(nr1.at[k, cc], a_ss.at[k, 4, cc], a_rs.at[k, 4, cc], dev(zm, cc))
            arrived(nr0.at[k, cc], a_ss.at[k, 5, cc], a_rs.at[k, 5, cc], dev(zp, cc))
        arrived(so.at[k], a_ss.at[k, 3, 0], a_rs.at[k, 3, 0], dev(z, sib))
        arrived(mg0.at[k], a_ss.at[k, 6, 0], a_rs.at[k, 6, 0], dev(zm, c))
        arrived(mg1.at[k], a_ss.at[k, 6, 1], a_rs.at[k, 6, 1], dev(zp, c))
        acc = jnp.zeros((8, 128), jnp.float32)
        for h, near, merged in ((0, nr0, mg0), (1, nr1, mg1)):
            def one(i, acc, h=h, near=near, merged=merged):
                inner = pl.ds(pl.multiple_of(i * step_rows, step_rows), step_rows)
                start = pl.multiple_of(h * half + i * step_rows, step_rows)
                at = pl.ds(start, step_rows)
                g = (f32(ownb[k, at]) + f32(so[k, at])) + (f32(near[k, 0, inner]) + f32(near[k, 1, inner])) + merged[k, inner]
                m = BETA_MOMENT * smv[k, at] + (1.0 - BETA_MOMENT) * g * g
                mom[k, at] = m
                a = g / (jnp.sqrt(m) + EPS_ADAM)
                gf[k, pl.ds(pl.multiple_of(r * band + start, step_rows), step_rows)] = g.astype(jnp.bfloat16)
                return acc + fold(a * a)

            acc = lax.fori_loop(0, half // step_rows, one, acc)
        nsend[k] = acc

    class Inward:
        def __init__(self, root, own, v0, sa, ra, sb, rb, sc, rc, ss, rs):
            self.root, self.own, self.v0 = root, own, v0
            self.bufs = [(sa, ra), (sb, rb), (sc, rc)]
            self.ss, self.rs = ss, rs

        def order(self, j):
            return [(j + i) % 4 for i in range(4)]

        def start(self):
            for j in range(Q):
                d = self.order(j)
                go(remote(self.root.at[:, pl.ds(part * j, part)], self.v0.at[j],
                          self.ss.at[0, j], self.rs.at[0, j], across(d[3])))

        def wait(self, stage):
            for j in range(Q):
                d = self.order(j)
                dst = self.v0.at[j] if stage == 0 else self.bufs[stage - 1][1].at[j]
                arrived(dst, self.ss.at[stage, j], self.rs.at[stage, j], across(d[3 - stage]))

        def pick(self, j, level, home_flips, k, ea, eb):
            d = self.order(j)
            place = inv_ref[2 * shard_at(home_flips) + k]
            owner, slot = place // NS, place % NS
            theirs = bits(owner)
            value = jnp.where(theirs[d[3]] != mine[d[3]], self.v0[j, slot],
                              self.own[slot, pl.ds(part * j, part)])
            if level >= 1:
                value = jnp.where(theirs[d[2]] != mine[d[2]], self.bufs[0][1][j, ea], value)
            if level >= 2:
                value = jnp.where(theirs[d[1]] != mine[d[1]], self.bufs[1][1][j, eb], value)
            if level >= 3:
                value = jnp.where(theirs[d[0]] != mine[d[0]], self.bufs[2][1][j, k], value)
            return value

        def send(self, stage):
            src, dst = self.bufs[stage - 1]
            for j in range(Q):
                d = self.order(j)
                for e in range(8 >> (stage - 1)):
                    k, r0, r1 = e % 2, (e // 2) % 2, e // 4
                    if stage == 1:
                        flips = (d[2],) + ((d[0],) if r0 else ()) + ((d[1],) if r1 else ())
                        ea = eb = None
                    elif stage == 2:
                        flips = (d[1],) + ((d[0],) if r0 else ())
                        ea, eb = 4 + 2 * r0 + k, None
                    else:
                        flips = (d[0],)
                        ea, eb = 2 + k, 2 + k
                    src[j, e] = self.pick(j, stage - 1, flips, k, ea, eb)
                go(remote(src.at[j], dst.at[j], self.ss.at[stage, j], self.rs.at[stage, j], across(d[3 - stage])))

        def finish(self, put):
            for j in range(Q):
                for k in range(NK):
                    put(j, k, self.pick(j, 3, (), k, k, k))

    right = Inward(rroot, r_own, r_v0, r_sa, r_ra, r_sb, r_rb, r_sc, r_rc, rp_ss, rp_rs)
    left = Inward(lroot, l_own, l_v0, l_sa, l_ra, l_sb, l_rb, l_sc, l_rc, lp_ss, lp_rs)
    class Gather:
        def __init__(self, buf, ss, rs):
            self.buf, self.ss, self.rs = buf, ss, rs

        def copy(self, i, k, h, zz, cc, to):
            piece = self.buf.at[k, half_rows(zz, cc, h)]
            return remote(piece, piece, self.ss.at[i, k], self.rs.at[i, k], to)

        def got(self, i, k, h, zz, cc, to):
            self.copy(i, k, h, zz, cc, to).wait_recv()

        def start(self, k):
            go(self.copy(0, k, 0, z, c, dev(zm, c)))
            go(self.copy(1, k, 1, z, c, dev(zp, c)))
            go(self.copy(2, k, 1, z, c, dev(zm, c)))
            go(self.copy(3, k, 0, z, c, dev(zp, c)))
            go(self.copy(4, k, 0, z, c, dev(z, sib)))
            go(self.copy(5, k, 1, z, c, dev(z, sib)))

        def forward(self, k):
            self.got(0, k, 0, zp, c, dev(zm, c))
            go(self.copy(6, k, 0, zp, c, dev(zm, c)))
            self.got(1, k, 1, zm, c, dev(zp, c))
            go(self.copy(7, k, 1, zm, c, dev(zp, c)))
            go(self.copy(8, k, 0, zp, c, dev(z, sib)))
            go(self.copy(9, k, 1, zm, c, dev(z, sib)))

        def rest(self, k):
            self.got(2, k, 1, zp, c, dev(zm, c))
            go(self.copy(10, k, 1, zp, c, dev(z, sib)))
            self.got(3, k, 0, zm, c, dev(zp, c))
            go(self.copy(11, k, 0, zm, c, dev(z, sib)))

        def last(self, k):
            self.got(6, k, 0, zf, c, dev(zm, c))
            go(self.copy(12, k, 0, zf, c, dev(z, sib)))
            self.got(7, k, 1, zf, c, dev(zp, c))
            go(self.copy(13, k, 1, zf, c, dev(z, sib)))

        def complete(self, k):
            for i, h, zz in ((4, 0, z), (5, 1, z), (8, 0, zp), (9, 1, zm), (10, 1, zp), (11, 0, zm), (12, 0, zf), (13, 1, zf)):
                self.got(i, k, h, zz, sib, dev(z, sib))

    gather_g = Gather(gf, gag_ss, gag_rs)
    gather_r = Gather(rf, rag_ss, rag_rs)

    def put_right(j, k, value):
        rf[k, pl.ds(pl.multiple_of(r * band + part * j, part), part)] = value

    def put_left(j, k, value):
        lh[k, pl.ds(part * j, part)] = value

    def column(t):
        return pl.ds(pl.multiple_of(((r + 8 + t) % 8) * TILE, TILE), TILE)

    class Outward:
        def __init__(self, held, src, dst, out, xs, xr, ss, rs, x_ss, x_rs):
            self.held, self.src, self.dst, self.out, self.ss, self.rs = held, src, dst, out, ss, rs
            self.xs, self.xr, self.x_ss, self.x_rs = xs, xr, x_ss, x_rs

        def order(self, j):
            return [(j + i) % 4 for i in range(4)]

        def spread(self, k, stage):
            n = 1 << stage
            for j in range(Q):
                d = self.order(j)
                go(remote(self.held.at[j, k, pl.ds(0, n)], self.held.at[j, k, pl.ds(n, n)],
                          self.ss.at[3 * k + stage, j], self.rs.at[3 * k + stage, j], across(d[stage])))

        def wait(self, k, stage):
            n = 1 << stage
            for j in range(Q):
                d = self.order(j)
                arrived(self.held.at[j, k, pl.ds(n, n)], self.ss.at[3 * k + stage, j], self.rs.at[3 * k + stage, j], across(d[stage]))

        def wait_last(self):
            for j in range(Q):
                d = self.order(j)
                arrived(self.dst.at[j], self.ss.at[6, j], self.rs.at[6, j], across(d[3]))

        def look(self, j, owner, q):
            d = self.order(j)
            block = ob_ref[owner * NS + q]
            safe = jnp.minimum(block, 31)
            theirs = bits(safe // 2)
            differ = [jnp.where(theirs[t] != mine[t], 1, 0) for t in d]
            return block, differ[3], self.held[j, safe % 2, differ[0] + 2 * differ[1] + 4 * differ[2]]

        def send(self):
            for j in range(Q):
                d = self.order(j)
                for q in range(NS):
                    self.src[j, q] = self.look(j, shard_at((d[3],)), q)[2]
                go(remote(self.src.at[j], self.dst.at[j], self.ss.at[6, j], self.rs.at[6, j], across(d[3])))

        def finish(self):
            for j in range(Q):
                for q in range(NS):
                    block, far, here = self.look(j, s, q)
                    value = jnp.where(far == 1, self.dst[j, q], here)
                    value = jnp.where(block < 32, value, jnp.zeros_like(value))
                    at = pl.ds(part * j, part)
                    for i, t in enumerate(TILES):
                        piece = value[:, TILE * i:TILE * (i + 1)]
                        self.out[q, at, column(t)] = piece
                        if i in SWAPPED:
                            self.xs[SWAPPED.index(i), q, at] = piece
            for i, t in enumerate(SWAPPED):
                go(remote(self.xs.at[i], self.xr.at[i], self.x_ss.at[i], self.x_rs.at[i], ((r + 8 + TILES[t]) % 8, s)))

        def swap(self):
            for i, t in enumerate(SWAPPED):
                arrived(self.xr.at[i], self.x_ss.at[i], self.x_rs.at[i], ((r + 8 + TILES[t]) % 8, s))
                for q in range(NS):
                    self.out[q, :, column(-TILES[t])] = self.xr[i, q].T

    out_l = Outward(gl_h, gl_s, gl_r, gl_o, gl_xs, gl_xr, glp_ss, glp_rs, xl_ss, xl_rs)
    out_r = Outward(gr_h, gr_s, gr_r, gr_o, gr_xs, gr_xr, grp_ss, grp_rs, xr_ss, xr_rs)

    tile = 256
    mm = functools.partial(lax.dot_general, preferred_element_type=jnp.float32)

    def put_gram(held, k, i, g):
        g = g.astype(jnp.bfloat16)
        for j in range(Q):
            held[j, k, 0, :, pl.ds(TILE * i, TILE)] = g[part * j:part * (j + 1)]

    def gram_left(k):
        band_rows = gf[k, column(0)]
        for i, t in enumerate(TILES):
            put_gram(gl_h, k, i, mm(band_rows, gf[k, column(t)], (((1,), (1,)), ((), ()))))

    def gram_right(k):
        band_columns = gf[k, :, column(0)].T
        for i, t in enumerate(TILES):
            put_gram(gr_h, k, i, mm(band_columns, gf[k, :, column(t)], (((1,), (0,)), ((), ()))))

    def precondition(k):
        @pl.loop(0, width // tile)
        def _(i):
            at = pl.ds(pl.multiple_of(i * tile, tile), tile)
            tb[at] = mm(gf[k, at], rf[k], (((1,), (0,)), ((), ()))).astype(jnp.bfloat16)

        @pl.loop(0, width // tile)
        def _(i):
            at = pl.ds(pl.multiple_of(i * tile, tile), tile)
            pv[k, :, at] = mm(lh[k], tb[:, at], (((1,), (0,)), ((), ())))

        def square(i, acc):
            v = pv[k, pl.ds(pl.multiple_of(i * step_rows, step_rows), step_rows)]
            return acc + fold(v * v)

        nsend[NK + k] = lax.fori_loop(0, band // step_rows, square, jnp.zeros((8, 128), jnp.float32))

    others = [(z, sib, 0)] + [(zz, cc, 1 + 2 * i + cc) for i, zz in enumerate((zm, zp, zf)) for cc in (0, 1)]

    def norms_send():
        for zz, cc, i in others:
            go(remote(nsend, nrecv.at[r], n_ss.at[i], n_rs.at[r], dev(zz, cc)))

    def norms_apply():
        for zz, cc, i in others:
            src = zz * 2 + cc
            arrived(nrecv.at[src], n_ss.at[i], n_rs.at[src], dev(zz, cc))
        nrecv[r] = nsend[...]
        sums = nrecv[0]
        for i in range(1, 8):
            sums = sums + nrecv[i]
        for k in range(NK):
            adam_total = jnp.sum(sums[k], keepdims=True)
            pre_total = jnp.sum(sums[NK + k], keepdims=True)
            scaling = jnp.sqrt(adam_total) / (jnp.sqrt(pre_total) + EPS_NORM)

            @pl.loop(0, band // step_rows)
            def _(i, k=k, scaling=scaling):
                at = pl.ds(pl.multiple_of(i * step_rows, step_rows), step_rows)
                pv[k, at] = pv[k, at] * scaling

    mom_cp = pltpu.make_async_copy(mom, moment_out, loc_sem.at[6])
    up_cp = pltpu.make_async_copy(pv, update_out, loc_sem.at[7])
    gl_cp = pltpu.make_async_copy(gl_o, gl_out, loc_sem.at[8])
    gr_cp = pltpu.make_async_copy(gr_o, gr_out, loc_sem.at[9])

    far_send(0)
    side_send(0)
    near_send(0, 0)
    right.start()
    side_send(1)
    locs[0].wait()
    locs[1].wait()
    locs[4].wait()
    right.wait(0)
    right.send(1)
    left.start()
    far_wait(0)
    near_send(0, 1)
    merge(0)
    far_send(1)
    locs[5].wait()
    locs[2].wait()
    locs[3].wait()
    gradient(0)
    gather_g.start(0)
    near_send(1, 0)
    left.wait(0)
    left.send(1)
    right.wait(1)
    right.send(2)
    far_wait(1)
    merge(1)
    gather_g.forward(0)
    near_send(1, 1)
    gather_g.rest(0)
    gather_g.last(0)
    gradient(1)
    gather_g.start(1)
    mom_cp.start()
    gather_g.complete(0)
    gram_left(0)
    out_l.spread(0, 0)
    gram_right(0)
    out_r.spread(0, 0)
    right.wait(2)
    right.send(3)
    gather_g.forward(1)
    left.wait(1)
    left.send(2)
    gather_g.rest(1)
    out_l.wait(0, 0)
    out_l.spread(0, 1)
    out_r.wait(0, 0)
    out_r.spread(0, 1)
    gather_g.last(1)
    right.wait(3)
    right.finish(put_right)
    gather_r.start(0)
    out_l.wait(0, 1)
    out_l.spread(0, 2)
    out_r.wait(0, 1)
    out_r.spread(0, 2)
    gather_g.complete(1)
    gather_r.start(1)
    gram_left(1)
    out_l.spread(1, 0)
    gram_right(1)
    out_r.spread(1, 0)
    left.wait(2)
    left.send(3)
    gather_r.forward(0)
    out_l.wait(1, 0)
    out_l.spread(1, 1)
    out_r.wait(1, 0)
    out_r.spread(1, 1)
    gather_r.forward(1)
    gather_r.rest(0)
    gather_r.last(0)
    left.wait(3)
    left.finish(put_left)
    out_l.wait(1, 1)
    out_l.spread(1, 2)
    out_r.wait(1, 1)
    out_r.spread(1, 2)
    gather_r.rest(1)
    gather_r.last(1)
    gather_r.complete(0)
    precondition(0)
    out_l.wait(0, 2)
    out_r.wait(0, 2)
    out_l.wait(1, 2)
    out_l.send()
    out_r.wait(1, 2)
    out_r.send()
    gather_r.complete(1)
    precondition(1)
    norms_send()
    out_l.wait_last()
    out_l.finish()
    out_r.wait_last()
    out_r.finish()
    norms_apply()
    up_cp.start()
    out_l.swap()
    gl_cp.start()
    out_r.swap()
    gr_cp.start()

    for cp in sends:
        cp.wait_send()
    for cp in (mom_cp, up_cp, gl_cp, gr_cp):
        cp.wait()


def body(grads, second_moment, left_stats, right_stats, left_root, right_root, owner_blocks):
    bf16, f32 = jnp.bfloat16, jnp.float32
    band, width = second_moment.shape[1], second_moment.shape[2]
    full = 8 * band
    part = band // Q
    half = band // 2
    sent = len(TILES) * TILE
    table = owner_blocks.reshape(-1)
    blocks = jnp.arange(32, dtype=jnp.int32)
    inverse = jnp.sum(
        jnp.where(table[None, :] == blocks[:, None], jnp.arange(64, dtype=jnp.int32)[None, :], 0), axis=1
    )
    V, D = pltpu.VMEM, pltpu.SemaphoreType.DMA
    inward = [
        V((NS, band, width), bf16), V((Q, NS, part, width), bf16),
        V((Q, 8, part, width), bf16), V((Q, 8, part, width), bf16),
        V((Q, 4, part, width), bf16), V((Q, 4, part, width), bf16),
        V((Q, 2, part, width), bf16), V((Q, 2, part, width), bf16),
    ]
    outward = [
        V((Q, NK, 8, part, sent), bf16), V((Q, NS, part, sent), bf16),
        V((Q, NS, part, sent), bf16), V((NS, band, width), bf16),
        V((len(SWAPPED), NS, TILE, TILE), bf16), V((len(SWAPPED), NS, TILE, TILE), bf16),
    ]
    scratch = (
        [V((NK, 2, half, width), bf16)] * 2
        + [V((NK, half, width), bf16)] * 2
        + [V((NK, 2, half, width), bf16)] * 2
        + [V((NK, band, width), bf16)]
        + [V((NK, half, width), f32)] * 4
        + [V((NK, half, width), bf16)] * 2
        + [V((NK, band, width), bf16)]
        + [V((2, band, width), f32)] * 2
        + [V((2, full, width), bf16)] * 2
        + [V((full, width), bf16)]
        + [V((2, band, width), f32)]
        + [V((2, band, width), bf16)]
        + [V((4, 8, 128), f32), V((8, 4, 8, 128), f32)]
        + inward + inward + outward + outward
        + [D((10,)), D((NK, 7, 2)), D((NK, 7, 2))] + [D((14, 2))] * 4
        + [D((4, Q))] * 4
        + [D((7, Q))] * 4
        + [D((len(SWAPPED),))] * 4
        + [D((7,)), D((8,))]
    )
    hbm = pl.BlockSpec(memory_space=pl.ANY)
    smem = pl.BlockSpec(memory_space=pltpu.SMEM)
    update, moment_new, gram_left, gram_right = pl.pallas_call(
        kernel,
        out_shape=(
            jax.ShapeDtypeStruct((2, band, width), f32),
            jax.ShapeDtypeStruct((2, band, width), f32),
            jax.ShapeDtypeStruct((NS, band, width), bf16),
            jax.ShapeDtypeStruct((NS, band, width), bf16),
        ),
        in_specs=[smem, smem, hbm, hbm, hbm, hbm],
        out_specs=(hbm, hbm, hbm, hbm),
        scratch_shapes=scratch,
        compiler_params=pltpu.CompilerParams(
            collective_id=0, has_side_effects=True, vmem_limit_bytes=50 * 2**20
        ),
        name="shampoo",
    )(table, inverse, grads, second_moment, left_root, right_root)
    left_new = BETA_STAT * left_stats + (1.0 - BETA_STAT) * gram_left.astype(f32)
    right_new = BETA_STAT * right_stats + (1.0 - BETA_STAT) * gram_right.astype(f32)
    return (update, moment_new, left_new, right_new)


def solution(mesh):
    in_specs = (
        P("replica", "shard", None, None),
        P("shard", "replica", None),
        P("shard", "replica", None),
        P("shard", "replica", None),
        P("shard", "replica", None),
        P("shard", "replica", None),
        P(),
    )
    out_specs = (
        P("shard", "replica", None),
        P("shard", "replica", None),
        P("shard", "replica", None),
        P("shard", "replica", None),
    )
    return jax.shard_map(body, mesh=mesh, in_specs=in_specs, out_specs=out_specs, check_vma=False)
```

```python
import functools

import jax
import jax.numpy as jnp
from jax import lax
from jax.experimental import pallas as pl
from jax.experimental.pallas import tpu as pltpu
from jax.sharding import PartitionSpec as P

BETA_STAT = 0.99
BETA_MOMENT = 0.95
EPS_ADAM = 1e-08
EPS_NORM = 1e-06
MESH = pl.DeviceIdType.MESH

NS = 4
NK = 2
Q = 4
TILES = (0, 1, -2, 3, 4)
SWAPPED = (1, 2, 3)
TILE = 128


def flip(v, low, high):
    if low:
        v = v + 1 - 2 * (v % 2)
    if high:
        v = 3 - v
    return v


def gray_bits(v):
    return ((v + 1) // 2) % 2, v // 2


def kernel(
    ob_ref, inv_ref, grads, sm_hbm, lroot, rroot,
    update_out, moment_out, gl_out, gr_out,
    far0, far1, sm0, sm1, nr0, nr1, so, mg0, mg1, ms0, ms1, own0, own1, ownb,
    smv, mom, gf, rf, tb, pv, lh, nsend, nrecv,
    r_own, r_v0, r_sa, r_ra, r_sb, r_rb, r_sc, r_rc,
    l_own, l_v0, l_sa, l_ra, l_sb, l_rb, l_sc, l_rc,
    gl_h, gl_s, gl_r, gl_o, gl_xs, gl_xr, gr_h, gr_s, gr_r, gr_o, gr_xs, gr_xr,
    loc_sem, a_ss, a_rs, gag_ss, gag_rs, rag_ss, rag_rs,
    rp_ss, rp_rs, lp_ss, lp_rs, glp_ss, glp_rs, grp_ss, grp_rs, xl_ss, xl_rs, xr_ss, xr_rs, n_ss, n_rs,
):
    band = sm_hbm.shape[1]
    width = sm_hbm.shape[2]
    part = band // Q
    r = lax.axis_index("replica")
    s = lax.axis_index("shard")
    z, c = r // 2, r % 2
    x, y = s // 4, s % 4
    zp, zm, zf = (z + 1) % 4, (z + 3) % 4, (z + 2) % 4
    sib = 1 - c

    def dev(zz, cc):
        return (zz * 2 + cc, s)

    def rows(zz, cc):
        return pl.ds((zz * 2 + cc) * band, band)

    half = band // 2

    def half_rows(zz, cc, h):
        return pl.ds(pl.multiple_of((zz * 2 + cc) * band + h * half, half), half)

    def shard_at(flips):
        return 4 * flip(x, 2 in flips, 3 in flips) + flip(y, 0 in flips, 1 in flips)

    def across(dim):
        return (r, shard_at((dim,)))

    def bits(shard):
        ya, yb = gray_bits(shard % 4)
        xa, xb = gray_bits(shard // 4)
        return (ya, yb, xa, xb)

    mine = bits(s)

    def remote(src, dst, ss, rs, to):
        return pltpu.make_async_remote_copy(
            src_ref=src, dst_ref=dst, send_sem=ss, recv_sem=rs, device_id=to, device_id_type=MESH
        )

    me = (r, s)

    def arrived(dst, ss, rs, to):
        remote(dst, dst, ss, rs, to).wait_recv()

    sends = []

    def go(cp):
        cp.start()
        sends.append(cp)

    locs = [
        pltpu.make_async_copy(grads.at[0, :, half_rows(zm, c, 0)], own0, loc_sem.at[0]),
        pltpu.make_async_copy(grads.at[0, :, half_rows(zp, c, 1)], own1, loc_sem.at[1]),
        pltpu.make_async_copy(grads.at[0, :, rows(z, c)], ownb, loc_sem.at[2]),
        pltpu.make_async_copy(sm_hbm, smv, loc_sem.at[3]),
        pltpu.make_async_copy(rroot, r_own, loc_sem.at[4]),
        pltpu.make_async_copy(lroot, l_own, loc_sem.at[5]),
    ]
    for cp in locs:
        cp.start()

    barrier = pltpu.get_barrier_semaphore()
    partners = [dev(z, sib)] + [dev(zz, cc) for zz in (zm, zp, zf) for cc in (0, 1)]
    partners += [across(d) for d in range(4)]
    for p in partners:
        pl.semaphore_signal(barrier, inc=1, device_id=p, device_id_type=MESH)
    pl.semaphore_wait(barrier, len(partners))

    def far_send(k):
        for j in (0, 1):
            go(remote(grads.at[0, k, half_rows(zf, j, 0)], far0.at[k, c], a_ss.at[k, 0, j], a_rs.at[k, 0, c], dev(zm, j)))
            go(remote(grads.at[0, k, half_rows(zf, j, 1)], far1.at[k, c], a_ss.at[k, 1, j], a_rs.at[k, 1, c], dev(zp, j)))

    def side_send(k):
        go(remote(grads.at[0, k, half_rows(zm, sib, 0)], sm0.at[k], a_ss.at[k, 2, 0], a_rs.at[k, 2, 0], dev(z, sib)))
        go(remote(grads.at[0, k, half_rows(zp, sib, 1)], sm1.at[k], a_ss.at[k, 2, 1], a_rs.at[k, 2, 1], dev(z, sib)))
        go(remote(grads.at[0, k, rows(z, sib)], so.at[k], a_ss.at[k, 3, 0], a_rs.at[k, 3, 0], dev(z, sib)))

    def near_send(k, j):
        there = (c, sib)[j]
        go(remote(grads.at[0, k, half_rows(zm, there, 1)], nr1.at[k, c], a_ss.at[k, 4, j], a_rs.at[k, 4, c], dev(zm, there)))
        go(remote(grads.at[0, k, half_rows(zp, there, 0)], nr0.at[k, c], a_ss.at[k, 5, j], a_rs.at[k, 5, c], dev(zp, there)))

    step_rows = 16

    def f32(v):
        return v.astype(jnp.float32)

    def far_wait(k):
        for cc in (0, 1):
            arrived(far0.at[k, cc], a_ss.at[k, 0, cc], a_rs.at[k, 0, cc], dev(zm, cc))
            arrived(far1.at[k, cc], a_ss.at[k, 1, cc], a_rs.at[k, 1, cc], dev(zp, cc))
        arrived(sm0.at[k], a_ss.at[k, 2, 0], a_rs.at[k, 2, 0], dev(z, sib))
        arrived(sm1.at[k], a_ss.at[k, 2, 1], a_rs.at[k, 2, 1], dev(z, sib))

    def merge(k):
        @pl.loop(0, half // step_rows)
        def _(i):
            at = pl.ds(pl.multiple_of(i * step_rows, step_rows), step_rows)
            ms0[k, at] = (f32(own0[k, at]) + f32(sm0[k, at])) + (f32(far0[k, 0, at]) + f32(far0[k, 1, at]))
            ms1[k, at] = (f32(own1[k, at]) + f32(sm1[k, at])) + (f32(far1[k, 0, at]) + f32(far1[k, 1, at]))

        go(remote(ms0.at[k], mg0.at[k], a_ss.at[k, 6, 0], a_rs.at[k, 6, 0], dev(zm, c)))
        go(remote(ms1.at[k], mg1.at[k], a_ss.at[k, 6, 1], a_rs.at[k, 6, 1], dev(zp, c)))

    def fold(v):
        v = v[:8] + v[8:]
        total = v[:, :128]
        for i in range(1, width // 128):
            total = total + v[:, 128 * i:128 * (i + 1)]
        return total

    def gradient(k):
        for cc in (0, 1):
            arrived(nr1.at[k, cc], a_ss.at[k, 4, cc], a_rs.at[k, 4, cc], dev(zm, cc))
            arrived(nr0.at[k, cc], a_ss.at[k, 5, cc], a_rs.at[k, 5, cc], dev(zp, cc))
        arrived(so.at[k], a_ss.at[k, 3, 0], a_rs.at[k, 3, 0], dev(z, sib))
        arrived(mg0.at[k], a_ss.at[k, 6, 0], a_rs.at[k, 6, 0], dev(zm, c))
        arrived(mg1.at[k], a_ss.at[k, 6, 1], a_rs.at[k, 6, 1], dev(zp, c))
        acc = jnp.zeros((8, 128), jnp.float32)
        for h, near, merged in ((0, nr0, mg0), (1, nr1, mg1)):
            def one(i, acc, h=h, near=near, merged=merged):
                inner = pl.ds(pl.multiple_of(i * step_rows, step_rows), step_rows)
                start = pl.multiple_of(h * half + i * step_rows, step_rows)
                at = pl.ds(start, step_rows)
                g = (f32(ownb[k, at]) + f32(so[k, at])) + (f32(near[k, 0, inner]) + f32(near[k, 1, inner])) + merged[k, inner]
                m = BETA_MOMENT * smv[k, at] + (1.0 - BETA_MOMENT) * g * g
                mom[k, at] = m
                a = g / (jnp.sqrt(m) + EPS_ADAM)
                gf[k, pl.ds(pl.multiple_of(r * band + start, step_rows), step_rows)] = g.astype(jnp.bfloat16)
                return acc + fold(a * a)

            acc = lax.fori_loop(0, half // step_rows, one, acc)
        nsend[k] = acc

    class Inward:
        def __init__(self, root, own, v0, sa, ra, sb, rb, sc, rc, ss, rs):
            self.root, self.own, self.v0 = root, own, v0
            self.bufs = [(sa, ra), (sb, rb), (sc, rc)]
            self.ss, self.rs = ss, rs

        def order(self, j):
            return [(j + i) % 4 for i in range(4)]

        def start(self):
            for j in range(Q):
                d = self.order(j)
                go(remote(self.root.at[:, pl.ds(part * j, part)], self.v0.at[j],
                          self.ss.at[0, j], self.rs.at[0, j], across(d[3])))

        def wait(self, stage):
            for j in range(Q):
                d = self.order(j)
                dst = self.v0.at[j] if stage == 0 else self.bufs[stage - 1][1].at[j]
                arrived(dst, self.ss.at[stage, j], self.rs.at[stage, j], across(d[3 - stage]))

        def pick(self, j, level, home_flips, k, ea, eb):
            d = self.order(j)
            place = inv_ref[2 * shard_at(home_flips) + k]
            owner, slot = place // NS, place % NS
            theirs = bits(owner)
            value = jnp.where(theirs[d[3]] != mine[d[3]], self.v0[j, slot],
                              self.own[slot, pl.ds(part * j, part)])
            if level >= 1:
                value = jnp.where(theirs[d[2]] != mine[d[2]], self.bufs[0][1][j, ea], value)
            if level >= 2:
                value = jnp.where(theirs[d[1]] != mine[d[1]], self.bufs[1][1][j, eb], value)
            if level >= 3:
                value = jnp.where(theirs[d[0]] != mine[d[0]], self.bufs[2][1][j, k], value)
            return value

        def send(self, stage):
            src, dst = self.bufs[stage - 1]
            for j in range(Q):
                d = self.order(j)
                for e in range(8 >> (stage - 1)):
                    k, r0, r1 = e % 2, (e // 2) % 2, e // 4
                    if stage == 1:
                        flips = (d[2],) + ((d[0],) if r0 else ()) + ((d[1],) if r1 else ())
                        ea = eb = None
                    elif stage == 2:
                        flips = (d[1],) + ((d[0],) if r0 else ())
                        ea, eb = 4 + 2 * r0 + k, None
                    else:
                        flips = (d[0],)
                        ea, eb = 2 + k, 2 + k
                    src[j, e] = self.pick(j, stage - 1, flips, k, ea, eb)
                go(remote(src.at[j], dst.at[j], self.ss.at[stage, j], self.rs.at[stage, j], across(d[3 - stage])))

        def finish(self, put):
            for j in range(Q):
                for k in range(NK):
                    put(j, k, self.pick(j, 3, (), k, k, k))

    right = Inward(rroot, r_own, r_v0, r_sa, r_ra, r_sb, r_rb, r_sc, r_rc, rp_ss, rp_rs)
    left = Inward(lroot, l_own, l_v0, l_sa, l_ra, l_sb, l_rb, l_sc, l_rc, lp_ss, lp_rs)
    class Gather:
        def __init__(self, buf, ss, rs):
            self.buf, self.ss, self.rs = buf, ss, rs

        def copy(self, i, k, h, zz, cc, to):
            piece = self.buf.at[k, half_rows(zz, cc, h)]
            return remote(piece, piece, self.ss.at[i, k], self.rs.at[i, k], to)

        def got(self, i, k, h, zz, cc, to):
            self.copy(i, k, h, zz, cc, to).wait_recv()

        def start(self, k):
            go(self.copy(0, k, 0, z, c, dev(zm, c)))
            go(self.copy(1, k, 1, z, c, dev(zp, c)))
            go(self.copy(2, k, 1, z, c, dev(zm, c)))
            go(self.copy(3, k, 0, z, c, dev(zp, c)))
            go(self.copy(4, k, 0, z, c, dev(z, sib)))
            go(self.copy(5, k, 1, z, c, dev(z, sib)))

        def forward(self, k):
            self.got(0, k, 0, zp, c, dev(zm, c))
            go(self.copy(6, k, 0, zp, c, dev(zm, c)))
            self.got(1, k, 1, zm, c, dev(zp, c))
            go(self.copy(7, k, 1, zm, c, dev(zp, c)))
            go(self.copy(8, k, 0, zp, c, dev(z, sib)))
            go(self.copy(9, k, 1, zm, c, dev(z, sib)))

        def rest(self, k):
            self.got(2, k, 1, zp, c, dev(zm, c))
            go(self.copy(10, k, 1, zp, c, dev(z, sib)))
            self.got(3, k, 0, zm, c, dev(zp, c))
            go(self.copy(11, k, 0, zm, c, dev(z, sib)))

        def last(self, k):
            self.got(6, k, 0, zf, c, dev(zm, c))
            go(self.copy(12, k, 0, zf, c, dev(z, sib)))
            self.got(7, k, 1, zf, c, dev(zp, c))
            go(self.copy(13, k, 1, zf, c, dev(z, sib)))

        def complete(self, k):
            for i, h, zz in ((4, 0, z), (5, 1, z), (8, 0, zp), (9, 1, zm), (10, 1, zp), (11, 0, zm), (12, 0, zf), (13, 1, zf)):
                self.got(i, k, h, zz, sib, dev(z, sib))

    gather_g = Gather(gf, gag_ss, gag_rs)
    gather_r = Gather(rf, rag_ss, rag_rs)

    def put_right(j, k, value):
        rf[k, pl.ds(pl.multiple_of(r * band + part * j, part), part)] = value

    def put_left(j, k, value):
        lh[k, pl.ds(part * j, part)] = value

    def column(t):
        return pl.ds(pl.multiple_of(((r + 8 + t) % 8) * TILE, TILE), TILE)

    class Outward:
        def __init__(self, held, src, dst, out, xs, xr, ss, rs, x_ss, x_rs):
            self.held, self.src, self.dst, self.out, self.ss, self.rs = held, src, dst, out, ss, rs
            self.xs, self.xr, self.x_ss, self.x_rs = xs, xr, x_ss, x_rs

        def order(self, j):
            return [(j + i) % 4 for i in range(4)]

        def spread(self, k, stage):
            n = 1 << stage
            for j in range(Q):
                d = self.order(j)
                go(remote(self.held.at[j, k, pl.ds(0, n)], self.held.at[j, k, pl.ds(n, n)],
                          self.ss.at[3 * k + stage, j], self.rs.at[3 * k + stage, j], across(d[stage])))

        def wait(self, k, stage):
            n = 1 << stage
            for j in range(Q):
                d = self.order(j)
                arrived(self.held.at[j, k, pl.ds(n, n)], self.ss.at[3 * k + stage, j], self.rs.at[3 * k + stage, j], across(d[stage]))

        def wait_last(self):
            for j in range(Q):
                d = self.order(j)
                arrived(self.dst.at[j], self.ss.at[6, j], self.rs.at[6, j], across(d[3]))

        def look(self, j, owner, q):
            d = self.order(j)
            block = ob_ref[owner * NS + q]
            safe = jnp.minimum(block, 31)
            theirs = bits(safe // 2)
            differ = [jnp.where(theirs[t] != mine[t], 1, 0) for t in d]
            return block, differ[3], self.held[j, safe % 2, differ[0] + 2 * differ[1] + 4 * differ[2]]

        def send(self):
            for j in range(Q):
                d = self.order(j)
                for q in range(NS):
                    self.src[j, q] = self.look(j, shard_at((d[3],)), q)[2]
                go(remote(self.src.at[j], self.dst.at[j], self.ss.at[6, j], self.rs.at[6, j], across(d[3])))

        def finish(self):
            for j in range(Q):
                for q in range(NS):
                    block, far, here = self.look(j, s, q)
                    value = jnp.where(far == 1, self.dst[j, q], here)
                    value = jnp.where(block < 32, value, jnp.zeros_like(value))
                    at = pl.ds(part * j, part)
                    for i, t in enumerate(TILES):
                        piece = value[:, TILE * i:TILE * (i + 1)]
                        self.out[q, at, column(t)] = piece
                        if i in SWAPPED:
                            self.xs[SWAPPED.index(i), q, at] = piece
            for i, t in enumerate(SWAPPED):
                go(remote(self.xs.at[i], self.xr.at[i], self.x_ss.at[i], self.x_rs.at[i], ((r + 8 + TILES[t]) % 8, s)))

        def swap(self):
            for i, t in enumerate(SWAPPED):
                arrived(self.xr.at[i], self.x_ss.at[i], self.x_rs.at[i], ((r + 8 + TILES[t]) % 8, s))
                for q in range(NS):
                    self.out[q, :, column(-TILES[t])] = self.xr[i, q].T

    out_l = Outward(gl_h, gl_s, gl_r, gl_o, gl_xs, gl_xr, glp_ss, glp_rs, xl_ss, xl_rs)
    out_r = Outward(gr_h, gr_s, gr_r, gr_o, gr_xs, gr_xr, grp_ss, grp_rs, xr_ss, xr_rs)

    tile = 256
    mm = functools.partial(lax.dot_general, preferred_element_type=jnp.float32)

    def put_gram(held, k, i, g):
        g = g.astype(jnp.bfloat16)
        for j in range(Q):
            held[j, k, 0, :, pl.ds(TILE * i, TILE)] = g[part * j:part * (j + 1)]

    def gram_left(k):
        band_rows = gf[k, column(0)]
        for i, t in enumerate(TILES):
            put_gram(gl_h, k, i, mm(band_rows, gf[k, column(t)], (((1,), (1,)), ((), ()))))

    def gram_right(k):
        band_columns = gf[k, :, column(0)].T
        for i, t in enumerate(TILES):
            put_gram(gr_h, k, i, mm(band_columns, gf[k, :, column(t)], (((1,), (0,)), ((), ()))))

    def precondition(k):
        @pl.loop(0, 4)
        def _(i):
            at = pl.ds(pl.multiple_of((i // 2) * 512, 512), 512)
            columns = pl.ds(pl.multiple_of((i % 2) * 512, 512), 512)
            tb[at, columns] = mm(gf[k, at], rf[k, :, columns], (((1,), (0,)), ((), ()))).astype(jnp.bfloat16)

        @pl.loop(0, width // tile)
        def _(i):
            at = pl.ds(pl.multiple_of(i * tile, tile), tile)
            pv[k, :, at] = mm(lh[k], tb[:, at], (((1,), (0,)), ((), ())))

        def square(i, acc):
            v = pv[k, pl.ds(pl.multiple_of(i * step_rows, step_rows), step_rows)]
            return acc + fold(v * v)

        nsend[NK + k] = lax.fori_loop(0, band // step_rows, square, jnp.zeros((8, 128), jnp.float32))

    others = [(z, sib, 0)] + [(zz, cc, 1 + 2 * i + cc) for i, zz in enumerate((zm, zp, zf)) for cc in (0, 1)]

    def norms_send():
        for zz, cc, i in others:
            go(remote(nsend, nrecv.at[r], n_ss.at[i], n_rs.at[r], dev(zz, cc)))

    def norms_apply():
        for zz, cc, i in others:
            src = zz * 2 + cc
            arrived(nrecv.at[src], n_ss.at[i], n_rs.at[src], dev(zz, cc))
        nrecv[r] = nsend[...]
        sums = nrecv[0]
        for i in range(1, 8):
            sums = sums + nrecv[i]
        for k in range(NK):
            adam_total = jnp.sum(sums[k], keepdims=True)
            pre_total = jnp.sum(sums[NK + k], keepdims=True)
            scaling = jnp.sqrt(adam_total) / (jnp.sqrt(pre_total) + EPS_NORM)

            @pl.loop(0, band // step_rows)
            def _(i, k=k, scaling=scaling):
                at = pl.ds(pl.multiple_of(i * step_rows, step_rows), step_rows)
                pv[k, at] = pv[k, at] * scaling

    mom_cp = pltpu.make_async_copy(mom, moment_out, loc_sem.at[6])
    up_cp = pltpu.make_async_copy(pv, update_out, loc_sem.at[7])
    gl_cp = pltpu.make_async_copy(gl_o, gl_out, loc_sem.at[8])
    gr_cp = pltpu.make_async_copy(gr_o, gr_out, loc_sem.at[9])

    far_send(0)
    side_send(0)
    near_send(0, 0)
    right.start()
    side_send(1)
    locs[0].wait()
    locs[1].wait()
    locs[4].wait()
    right.wait(0)
    right.send(1)
    left.start()
    far_wait(0)
    near_send(0, 1)
    merge(0)
    far_send(1)
    locs[5].wait()
    locs[2].wait()
    locs[3].wait()
    gradient(0)
    gather_g.start(0)
    near_send(1, 0)
    left.wait(0)
    left.send(1)
    right.wait(1)
    right.send(2)
    far_wait(1)
    merge(1)
    gather_g.forward(0)
    near_send(1, 1)
    gather_g.rest(0)
    gather_g.last(0)
    gradient(1)
    gather_g.start(1)
    mom_cp.start()
    gather_g.complete(0)
    gram_left(0)
    out_l.spread(0, 0)
    gram_right(0)
    out_r.spread(0, 0)
    right.wait(2)
    right.send(3)
    gather_g.forward(1)
    left.wait(1)
    left.send(2)
    gather_g.rest(1)
    out_l.wait(0, 0)
    out_l.spread(0, 1)
    out_r.wait(0, 0)
    out_r.spread(0, 1)
    gather_g.last(1)
    right.wait(3)
    right.finish(put_right)
    gather_r.start(0)
    out_l.wait(0, 1)
    out_l.spread(0, 2)
    out_r.wait(0, 1)
    out_r.spread(0, 2)
    gather_g.complete(1)
    gather_r.start(1)
    gram_left(1)
    out_l.spread(1, 0)
    gram_right(1)
    out_r.spread(1, 0)
    left.wait(2)
    left.send(3)
    gather_r.forward(0)
    out_l.wait(1, 0)
    out_l.spread(1, 1)
    out_r.wait(1, 0)
    out_r.spread(1, 1)
    gather_r.forward(1)
    gather_r.rest(0)
    gather_r.last(0)
    left.wait(3)
    left.finish(put_left)
    out_l.wait(1, 1)
    out_l.spread(1, 2)
    out_r.wait(1, 1)
    out_r.spread(1, 2)
    gather_r.rest(1)
    gather_r.last(1)
    gather_r.complete(0)
    precondition(0)
    out_l.wait(0, 2)
    out_r.wait(0, 2)
    out_l.wait(1, 2)
    out_l.send()
    out_r.wait(1, 2)
    out_r.send()
    gather_r.complete(1)
    precondition(1)
    norms_send()
    out_l.wait_last()
    out_l.finish()
    out_r.wait_last()
    out_r.finish()
    norms_apply()
    up_cp.start()
    out_l.swap()
    gl_cp.start()
    out_r.swap()
    gr_cp.start()

    for cp in sends:
        cp.wait_send()
    for cp in (mom_cp, up_cp, gl_cp, gr_cp):
        cp.wait()


def body(grads, second_moment, left_stats, right_stats, left_root, right_root, owner_blocks):
    bf16, f32 = jnp.bfloat16, jnp.float32
    band, width = second_moment.shape[1], second_moment.shape[2]
    full = 8 * band
    part = band // Q
    half = band // 2
    sent = len(TILES) * TILE
    table = owner_blocks.reshape(-1)
    blocks = jnp.arange(32, dtype=jnp.int32)
    inverse = jnp.sum(
        jnp.where(table[None, :] == blocks[:, None], jnp.arange(64, dtype=jnp.int32)[None, :], 0), axis=1
    )
    V, D = pltpu.VMEM, pltpu.SemaphoreType.DMA
    inward = [
        V((NS, band, width), bf16), V((Q, NS, part, width), bf16),
        V((Q, 8, part, width), bf16), V((Q, 8, part, width), bf16),
        V((Q, 4, part, width), bf16), V((Q, 4, part, width), bf16),
        V((Q, 2, part, width), bf16), V((Q, 2, part, width), bf16),
    ]
    outward = [
        V((Q, NK, 8, part, sent), bf16), V((Q, NS, part, sent), bf16),
        V((Q, NS, part, sent), bf16), V((NS, band, width), bf16),
        V((len(SWAPPED), NS, TILE, TILE), bf16), V((len(SWAPPED), NS, TILE, TILE), bf16),
    ]
    scratch = (
        [V((NK, 2, half, width), bf16)] * 2
        + [V((NK, half, width), bf16)] * 2
        + [V((NK, 2, half, width), bf16)] * 2
        + [V((NK, band, width), bf16)]
        + [V((NK, half, width), f32)] * 4
        + [V((NK, half, width), bf16)] * 2
        + [V((NK, band, width), bf16)]
        + [V((2, band, width), f32)] * 2
        + [V((2, full, width), bf16)] * 2
        + [V((full, width), bf16)]
        + [V((2, band, width), f32)]
        + [V((2, band, width), bf16)]
        + [V((4, 8, 128), f32), V((8, 4, 8, 128), f32)]
        + inward + inward + outward + outward
        + [D((10,)), D((NK, 7, 2)), D((NK, 7, 2))] + [D((14, 2))] * 4
        + [D((4, Q))] * 4
        + [D((7, Q))] * 4
        + [D((len(SWAPPED),))] * 4
        + [D((7,)), D((8,))]
    )
    hbm = pl.BlockSpec(memory_space=pl.ANY)
    smem = pl.BlockSpec(memory_space=pltpu.SMEM)
    update, moment_new, gram_left, gram_right = pl.pallas_call(
        kernel,
        out_shape=(
            jax.ShapeDtypeStruct((2, band, width), f32),
            jax.ShapeDtypeStruct((2, band, width), f32),
            jax.ShapeDtypeStruct((NS, band, width), bf16),
            jax.ShapeDtypeStruct((NS, band, width), bf16),
        ),
        in_specs=[smem, smem, hbm, hbm, hbm, hbm],
        out_specs=(hbm, hbm, hbm, hbm),
        scratch_shapes=scratch,
        compiler_params=pltpu.CompilerParams(
            collective_id=0, has_side_effects=True, vmem_limit_bytes=50 * 2**20
        ),
        name="shampoo",
    )(table, inverse, grads, second_moment, left_root, right_root)
    left_new = BETA_STAT * left_stats + (1.0 - BETA_STAT) * gram_left.astype(f32)
    right_new = BETA_STAT * right_stats + (1.0 - BETA_STAT) * gram_right.astype(f32)
    return (update, moment_new, left_new, right_new)


def solution(mesh):
    in_specs = (
        P("replica", "shard", None, None),
        P("shard", "replica", None),
        P("shard", "replica", None),
        P("shard", "replica", None),
        P("shard", "replica", None),
        P("shard", "replica", None),
        P(),
    )
    out_specs = (
        P("shard", "replica", None),
        P("shard", "replica", None),
        P("shard", "replica", None),
        P("shard", "replica", None),
    )
    return jax.shard_map(body, mesh=mesh, in_specs=in_specs, out_specs=out_specs, check_vma=False)
```
